768 devices in a mesh: dom: 16 (over y, core), grp: 48 (over z, x).
Axes of the slice: x: 4, y: 8, z: 12, core: 2. Of those that a mesh axis runs over, the one named last changes fastest.
Arguments:
- features: bfloat16 [196608, 256], P(('dom', 'grp')), may hold values from -6 to 6
- w_self: bfloat16 [256, 256], replicated, may hold values from -0.375 to 0.375
- w_neigh: bfloat16 [256, 256], replicated, may hold values from -9 to 9
- adjacency: bfloat16 [1536, 8, 128, 128], P(('dom', 'grp')), may hold values from 0 to 1
- tile_ids: int32 [1536, 8], P(('dom', 'grp')), may hold values from 0 to 11
- send_rows: int32 [12288, 32], P(('dom', 'grp')), may hold values from 0 to 255
- send_counts: int32 [768, 16], P(('dom', 'grp')), may hold values from 1 to 32, 256 in all within a row
- hub_rows: int32 [768, 16], P(('dom', 'grp')), may hold values from 0 to 255
- cotangent: bfloat16 [196608, 256], P(('dom', 'grp')), may hold values from -6 to 6
Outputs:
- output: bfloat16 [196608, 256], P(('dom', 'grp'))
- grad_features: bfloat16 [196608, 256], P(('dom', 'grp'))
- grad_self: float32 [256, 256], replicated
- grad_neigh: float32 [256, 256], replicated
The draws below stay inside these ranges and needn't reach their ends.
Inputs may be any that keep to these rules, and one draw needn't show every extreme that they name: `send_counts`: each device's counts to the 16 partitions sum to 256; on every device one count is exactly 32. `send_rows`: rows may repeat within a list. `hub_rows`: rows may repeat. `tile_ids`: A column tile may be read by several stored tiles or by none.
All inputs are finite; a program needn't handle non-finite values.
Results may differ from the reference program's by a relative error of at most 0.0057.
Values may be sent and summed in bfloat16 or wider, within the bound.
A program may use at most 32 MiB of HBM per device.

```python
import math
import jax
import jax.numpy as jnp
import numpy as np
from jax import lax

F = 256
H = 256
NODE_DEV = 256
TILE = 128
TPR = 8
SEND = 32
HUB_DEV = 16
ROW_TILES = 2
SRC_TILES = 12
NODES = 196608
N_DOM = 16
N_GRP = 48


def set_ends(entries, stream_key, least, high):
    longest = entries.shape.index(max(entries.shape))
    spots = []
    for shift in (0, 1):
        where = [jax.random.randint(jax.random.fold_in(stream_key, axis), (), 0, length) for axis, length in enumerate(entries.shape)]
        where[longest] = (where[longest] + shift) % entries.shape[longest]
        spots.append(tuple(where))
    return entries.at[spots[0]].set(least).at[spots[1]].set(high)


def block_levels(own_key, dims, cuts, low, top_value):
    level = 1.0
    for position, shards_of in cuts:
        draws = jax.random.uniform(jax.random.fold_in(jax.random.fold_in(own_key, 6), position), (shards_of,), jnp.float32, low / len(cuts), top_value / len(cuts))
        level = level * jnp.repeat(jnp.exp(draws), dims[position] // shards_of).reshape((-1,) + (1,) * (len(dims) - 1 - position))
    return level


def split_up(count, total, reach, skew):
    loads = [(1 << 20) // math.isqrt(standing ** skew) + 1 for standing in range(2, count + 1)]
    spare, holding = total - reach - (count - 1), [1] * (count - 1)
    while spare > 0:
        free = [i for i in range(count - 1) if holding[i] < reach]
        pool, left = sum([loads[i] for i in free]), spare
        for i in free:
            addition = min(reach - holding[i], max(1, left * loads[i] // pool), spare)
            holding[i] = holding[i] + addition
            spare = spare - addition
    return np.array([reach] + holding)


def uneven(stream_key, amount, total, reach, skew):
    if amount == 2:
        one = jax.random.randint(stream_key, (), max(1, total - reach), min(reach, total - 1) + 1)
        return jnp.stack([one, total - one])
    lengths = jnp.asarray(split_up(amount, total, reach, skew), jnp.int32)
    twos = (amount - 1) // 2
    source_of, taker = lengths[1:1 + 2 * twos:2], lengths[2:2 + 2 * twos:2]
    room = jnp.minimum(source_of - 1, reach - taker)
    shifted = jax.random.randint(jax.random.fold_in(stream_key, 1), (twos,), 0, 1 << 20) % (room + 1)
    lengths = lengths.at[1:1 + 2 * twos:2].set(source_of - shifted).at[2:2 + 2 * twos:2].set(taker + shifted)
    return lengths[jax.random.permutation(jax.random.fold_in(stream_key, 2), amount)]


def bell_draw(stream_key, shape, width, reach, pieces=(), kind=jnp.bfloat16):
    array = jax.random.normal(stream_key, shape, jnp.float32) * width
    if len(pieces) > 0:
        array = block_levels(stream_key, shape, pieces, -0.22, 0.18) * array
    return jnp.clip(array, min=-reach, max=reach).astype(kind)


def setup_inputs(seed: int = 0) -> dict:
    streams_of = jax.random.split(jax.random.key(seed), 10)
    return {
        "features": bell_draw(streams_of[0], (NODES, F), 1.0, 6.0, ((0, 768),)),
        "w_self": bell_draw(streams_of[1], (F, H), F ** -0.5, 0.375),
        "w_neigh": bell_draw(streams_of[2], (F, H), 1.5, 9.0),
        "adjacency": jnp.clip(1.0 * jax.random.uniform(streams_of[3], (N_DOM * N_GRP * ROW_TILES, TPR, TILE, TILE), jnp.float32) ** block_levels(streams_of[3], (N_DOM * N_GRP * ROW_TILES, TPR, TILE, TILE), ((0, 768),), -0.2, 0.2), 0.0, 1.0).astype(jnp.bfloat16),
        "tile_ids": set_ends(jax.random.randint(streams_of[4], (N_DOM * N_GRP * ROW_TILES, TPR), 0, SRC_TILES), jax.random.fold_in(streams_of[4], 1), 0, SRC_TILES - 1).astype(jnp.int32),
        "send_rows": set_ends(jax.random.randint(streams_of[5], (N_DOM * N_GRP * N_DOM, SEND), 0, NODE_DEV), jax.random.fold_in(streams_of[5], 1), 0, NODE_DEV - 1).astype(jnp.int32),
        "send_counts": jax.vmap(lambda own: uneven(own, N_DOM, N_DOM * SEND // 2, SEND, 2))(jax.random.split(streams_of[6], (N_DOM * N_GRP))).reshape((N_DOM * N_GRP, N_DOM)).astype(jnp.int32),
        "hub_rows": set_ends(jax.random.randint(streams_of[7], (N_DOM * N_GRP, HUB_DEV), 0, NODE_DEV), jax.random.fold_in(streams_of[7], 1), 0, NODE_DEV - 1).astype(jnp.int32),
        "cotangent": bell_draw(streams_of[8], (NODES, H), 1.0, 6.0, ((0, 768),)),
    }


def local_layer(own_rows, halo_rows, hub_feats, adjacency, tile_index, w_self, w_neigh, cotangent):
    node_count, feat_width = own_rows.shape
    tile_size = adjacency.shape[2]
    source = jnp.concatenate([own_rows, halo_rows, hub_feats], axis=0)
    src_count = source.shape[0] // tile_size
    src_tiles = source.reshape(src_count, tile_size, feat_width)
    picked = src_tiles[tile_index]
    adj_wide = adjacency.astype(jnp.float32)
    numer = jnp.einsum('rtij,rtjf->rif', adj_wide, picked.astype(jnp.float32))
    denom = 1.0 + jnp.sum(adj_wide, axis=(1, 3))
    agg = (numer / denom[..., None]).reshape(node_count, feat_width).astype(jnp.bfloat16)
    preact = jnp.dot(own_rows, w_self, preferred_element_type=jnp.float32) + jnp.dot(agg, w_neigh, preferred_element_type=jnp.float32)
    sigmoid_pre = jax.nn.sigmoid(preact)
    output = (preact * sigmoid_pre).astype(jnp.bfloat16)
    grad_pre = (cotangent.astype(jnp.float32) * sigmoid_pre * (1.0 + preact * (1.0 - sigmoid_pre))).astype(jnp.bfloat16)
    grad_ws = jnp.dot(own_rows.T, grad_pre, preferred_element_type=jnp.float32)
    grad_wn = jnp.dot(agg.T, grad_pre, preferred_element_type=jnp.float32)
    grad_own = jnp.dot(grad_pre, w_self.T, preferred_element_type=jnp.float32)
    grad_agg = jnp.dot(grad_pre, w_neigh.T, preferred_element_type=jnp.float32)
    grad_num = (grad_agg.reshape(numer.shape) / denom[..., None]).astype(jnp.bfloat16)
    contrib = jnp.einsum('rtij,rif->rtjf', adj_wide, grad_num.astype(jnp.float32))
    grad_source = jnp.zeros((src_count, tile_size, feat_width), contrib.dtype).at[
        tile_index.reshape(-1)].add(contrib.reshape(-1, tile_size, feat_width)).reshape(-1, feat_width)
    halo_count = halo_rows.shape[0]
    return (output, grad_ws, grad_wn, grad_own + grad_source[:node_count],
            grad_source[node_count:node_count + halo_count], grad_source[node_count + halo_count:])


def reference(features, w_self, w_neigh, adjacency, tile_ids, send_rows, send_counts, hub_rows, cotangent):
    blocks = features.reshape(N_DOM, N_GRP, NODE_DEV, F)
    sends = send_rows.reshape(N_DOM, N_GRP, N_DOM, SEND)
    counts = send_counts.reshape(N_DOM, N_GRP, N_DOM)
    live_slots = jnp.arange(SEND, dtype=jnp.int32) < counts[..., None]

    def pick_sends(block_rows, slot_rows):
        return block_rows[slot_rows.reshape(-1)].reshape(N_DOM, SEND, F)

    sent = jax.vmap(jax.vmap(pick_sends))(blocks, sends)
    sent = jnp.where(live_slots[..., None], sent, jnp.zeros((), jnp.bfloat16))
    halo_all = sent.transpose(2, 1, 0, 3, 4).reshape(N_DOM * N_GRP, N_DOM * SEND, F)

    def pick_hubs(block_rows, slot_rows):
        return block_rows[slot_rows]

    hub_table = jax.vmap(jax.vmap(pick_hubs))(blocks, hub_rows.reshape(N_DOM, N_GRP, HUB_DEV))
    hub_table = hub_table.reshape(N_DOM, N_GRP * HUB_DEV, F)
    dom_index = jnp.arange(N_DOM * N_GRP, dtype=jnp.int32) // N_GRP

    def step(carry, inputs):
        own_rows, halo_rows, adj_dev, ids_dev, cot_dev, dom_dev = inputs
        result = local_layer(own_rows, halo_rows, hub_table[dom_dev], adj_dev, ids_dev, w_self, w_neigh, cot_dev)
        return (carry[0] + result[1], carry[1] + result[2]), (result[0], result[3], result[4], result[5])

    start = (jnp.zeros((F, H), jnp.float32), jnp.zeros((F, H), jnp.float32))
    inputs = (features.reshape(N_DOM * N_GRP, NODE_DEV, F), halo_all,
              adjacency.reshape(N_DOM * N_GRP, ROW_TILES, TPR, TILE, TILE),
              tile_ids.reshape(N_DOM * N_GRP, ROW_TILES, TPR),
              cotangent.reshape(N_DOM * N_GRP, NODE_DEV, H), dom_index)
    (grad_self, grad_neigh), (output, grad_own, grad_halo, grad_hub) = lax.scan(step, start, inputs)
    grad_halo = grad_halo.reshape(N_DOM, N_GRP, N_DOM, SEND, F).transpose(2, 1, 0, 3, 4)
    grad_halo = jnp.where(live_slots[..., None], grad_halo, jnp.zeros((), grad_halo.dtype))

    def add_rows(slot_rows, values):
        return jnp.zeros((NODE_DEV, F), values.dtype).at[slot_rows.reshape(-1)].add(values.reshape(-1, F))

    from_halo = jax.vmap(jax.vmap(add_rows))(sends, grad_halo)
    hub_sum = jnp.sum(grad_hub.reshape(N_DOM, N_GRP, N_GRP, HUB_DEV, F), axis=1)
    from_hubs = jax.vmap(jax.vmap(add_rows))(hub_rows.reshape(N_DOM, N_GRP, HUB_DEV), hub_sum)
    grad_total = grad_own.reshape(N_DOM, N_GRP, NODE_DEV, F) + from_halo + from_hubs
    return (output.reshape(NODES, H), grad_total.reshape(NODES, F).astype(jnp.bfloat16), grad_self, grad_neigh)
```

```python
import functools

import jax
import jax.numpy as jnp
from jax import lax
from jax.experimental import pallas as pl
from jax.experimental.pallas import tpu as pltpu
from jax.sharding import PartitionSpec as P

CORES = 2
X_CHIPS = 4

F32 = jnp.float32
BF16 = jnp.bfloat16


def mm(a, b):
    return jnp.dot(a, b, preferred_element_type=F32)


def mm_nt(a, b):
    return lax.dot_general(a, b, (((1,), (1,)), ((), ())), preferred_element_type=F32)


def nearest_first(count):
    order = []
    for k in range(1, count // 2 + 1):
        order.append(k)
        if count - k != k:
            order.append(count - k)
    return order


def kernel(
    dims,
    feat, w_self, w_neigh, adj, ids, send_rows, send_counts, hub_rows, cot,
    out, grad_feat, grad_self, grad_neigh,
    out_send, halo_in, hub_in, dense, dense_t, dense_low, dense_low_t, pick, pick_t, feat_t,
    g_send, g_ret, h_send, h_recv, h2_send, h2_recv,
    gw, w_sib, w2_send, w2_recv, w3_send, w3_recv, w4_recv, w_fin,
    halo_s, halo_r, hz_s, hz_r, hx_s, hx_r, gh_s, gh_r, gx_s, gx_r, gz_s, gz_r,
    w1_s, w1_r, w2_s, w2_r, w3_s, w3_r, w4_s, w4_r, w5_s, w5_r, w6_s, w6_r, w7_s, w7_r,
):
    nd, ny, nz, nx = dims
    nodes, width = feat.shape
    row_tiles, per_row, tile, _ = adj.shape
    slots = send_rows.shape[1]
    hubs = hub_rows.shape[1]
    src_tiles = dense.shape[0]
    own_tiles = nodes // tile
    halo_tiles = nd * slots // tile
    crows = w_fin.shape[3]
    me_d = lax.axis_index("dom")
    me_g = lax.axis_index("grp")
    y, core = lax.div(me_d, CORES), lax.rem(me_d, CORES)
    z, x = lax.div(me_g, nx), lax.rem(me_g, nx)

    def dom_at(k):
        return lax.rem(me_d + k, nd)

    def z_at(k):
        return lax.rem(z + k, nz)

    def x_at(k):
        return lax.rem(x + k, nx)

    def y_at(k):
        return lax.rem(y + k, ny)

    sibling = y * CORES + (1 - core)
    pending = []

    def push(src, dst, send_sem, recv_sem, d, g):
        copy = pltpu.make_async_remote_copy(
            src_ref=src, dst_ref=dst, send_sem=send_sem, recv_sem=recv_sem,
            device_id=(d, g), device_id_type=pl.DeviceIdType.MESH,
        )
        copy.start()
        pending.append(copy)
        return copy

    barrier = pltpu.get_barrier_semaphore()
    partners = [(dom_at(k), me_g) for k in range(1, nd)]
    partners += [(me_d, z_at(k) * nx + x) for k in range(1, nz)]
    partners += [(me_d, z * nx + x_at(k)) for k in range(1, nx)]
    for partner in partners:
        pl.semaphore_signal(barrier, inc=1, device_id=partner, device_id_type=pl.DeviceIdType.MESH)

    count_col = jnp.sum(
        jnp.where(
            lax.broadcasted_iota(jnp.int32, (nd, nd), 0) == lax.broadcasted_iota(jnp.int32, (nd, nd), 1),
            jnp.broadcast_to(send_counts[...], (nd, nd)), 0).astype(F32),
        axis=1, keepdims=True)
    live = lax.broadcasted_iota(jnp.int32, (nd, slots), 1).astype(F32) < count_col
    index = jnp.where(live, send_rows[...].astype(F32), -1.0)
    eye = lax.broadcasted_iota(jnp.int32, (slots, slots), 0) == lax.broadcasted_iota(jnp.int32, (slots, slots), 1)
    lane = lax.broadcasted_iota(jnp.int32, (slots, nodes), 1).astype(F32)
    for p in range(nd):
        column = jnp.sum(
            jnp.where(eye, jnp.broadcast_to(index[p:p + 1, :], (slots, slots)), 0.0), axis=1, keepdims=True)
        pick[p * slots:(p + 1) * slots, :] = jnp.where(lane == column, 1.0, 0.0).astype(BF16)
    hub_index = hub_rows[...].astype(F32)
    hub_eye = lax.broadcasted_iota(jnp.int32, (hubs, hubs), 0) == lax.broadcasted_iota(jnp.int32, (hubs, hubs), 1)
    hub_col = jnp.sum(
        jnp.where(hub_eye, jnp.broadcast_to(hub_index, (hubs, hubs)), 0.0), axis=1, keepdims=True)
    hub_pick = jnp.where(
        lax.broadcasted_iota(jnp.int32, (hubs, nodes), 1).astype(F32) == hub_col, 1.0, 0.0).astype(BF16)
    features = feat[...]
    hub_in[z, x] = mm(hub_pick, features).astype(BF16)
    out_send[...] = mm(pick[...], features).astype(BF16).reshape(nd, slots, width)
    halo_in[me_d] = out_send[me_d]

    pl.semaphore_wait(barrier, len(partners))

    near_z = nearest_first(nz)
    hub_z = {}
    for k in reversed(near_z):
        hub_z[k] = push(hub_in.at[z, x], hub_in.at[z, x], hz_s.at[k], hz_r.at[k], me_d, z_at(k) * nx + x)
    hub_x = []

    def forward(k):
        from_z = lax.rem(z + nz - k, nz)
        for j in range(1, nx):
            hub_x.append(push(
                hub_in.at[from_z, x], hub_in.at[from_z, x], hx_s.at[j, k], hx_r.at[j, k], me_d, z * nx + x_at(j)))

    forward(0)
    halo = []
    for k in range(1, nd):
        halo.append(push(
            out_send.at[dom_at(k)], halo_in.at[me_d], halo_s.at[k], halo_r.at[k], dom_at(k), me_g))

    def gather_tiles(c, carry):
        parts = []
        for r in range(row_tiles):
            total = jnp.zeros((tile, tile), F32)
            for t in range(per_row):
                total = total + jnp.where(ids[r, t] == c, adj[r, t].astype(F32), 0.0)
            parts.append(total)
        block = jnp.concatenate(parts, axis=0)
        high = block.astype(BF16)
        low = block - high.astype(F32)
        dense[c] = high
        dense_low[c] = low.astype(BF16)
        dense_t[c] = high.astype(F32).T.astype(BF16)
        dense_low_t[c] = low.T.astype(BF16)
        return carry

    lax.fori_loop(0, src_tiles, gather_tiles, 0)

    for k in near_z:
        hub_z[k].wait_recv()
        forward(k)

    sums = []
    for r in range(row_tiles):
        total = jnp.zeros((tile, tile), F32)
        for t in range(per_row):
            total = total + adj[r, t].astype(F32)
        sums.append(jnp.sum(total, axis=1, keepdims=True))
    inverse = 1.0 / (1.0 + jnp.concatenate(sums, axis=0))
    feat_t[...] = features.astype(F32).T.astype(BF16)
    pick_t[...] = pick[...].astype(F32).T.astype(BF16)

    def from_tiles(first, count, rows):
        return sum(
            mm(jnp.concatenate([part[c] for c in range(first, first + count)], axis=1), rows)
            for part in (dense, dense_low))

    def to_tiles(first, count, rows):
        return sum(
            mm(part[first:first + count].reshape(count * tile, nodes), rows) for part in (dense_t, dense_low_t))

    numer = from_tiles(0, own_tiles, features)
    pre = mm(features, w_self[...])
    for copy in halo:
        copy.wait_recv()
    numer = numer + from_tiles(own_tiles, halo_tiles, halo_in[...].reshape(nd * slots, width))
    for copy in hub_x:
        copy.wait_recv()
    hub_tiles = src_tiles - own_tiles - halo_tiles
    numer = numer + from_tiles(own_tiles + halo_tiles, hub_tiles, hub_in[...].reshape(nz * nx * hubs, width))
    agg = numer * inverse
    agg_b = agg.astype(BF16)
    pre = pre + mm(agg_b, w_neigh[...])
    sig = 1.0 / (1.0 + jnp.exp(-pre))
    out[...] = (pre * sig).astype(BF16)
    grad_pre = (cot[...].astype(F32) * sig * (1.0 + pre * (1.0 - sig))).astype(BF16)

    gw[0] = mm(feat_t[...], grad_pre)
    gw[1] = mm(agg_b.astype(F32).T.astype(BF16), grad_pre)
    w1 = push(gw.at[1 - core], w_sib, w1_s, w1_r, sibling, me_g)

    grad_num = (mm_nt(grad_pre, w_neigh[...]) * inverse).astype(BF16)
    hub_grad = to_tiles(own_tiles + halo_tiles, hub_tiles, grad_num).astype(BF16)
    for g in range(nz * nx):
        h_send[g % nx, g // nx] = hub_grad[g * hubs:(g + 1) * hubs, :]
    hub_gx = [
        push(h_send.at[x_at(j)], h_recv.at[x], gx_s.at[j], gx_r.at[j], me_d, z * nx + x_at(j)) for j in range(1, nx)]
    h_recv[x] = h_send[x]
    g_send[...] = to_tiles(own_tiles, halo_tiles, grad_num).astype(BF16).reshape(nd, slots, width)

    w1.wait_recv()
    mine = gw[core] + w_sib[...]
    yrows = nodes // ny
    for i in range(ny):
        for j in range(nx):
            top = i * yrows + (j // 2) * crows
            w2_send[i, j] = mine[top:top + crows, (j % 2) * 128:(j % 2) * 128 + 128].astype(BF16)
    w2 = [
        push(w2_send.at[y_at(k)], w2_recv.at[y], w2_s.at[k], w2_r.at[k], y_at(k) * CORES + core, me_g)
        for k in range(1, ny)]
    w2_recv[y] = w2_send[y]
    ret = [
        push(g_send.at[dom_at(k)], g_ret.at[me_d], gh_s.at[k], gh_r.at[k], dom_at(k), me_g) for k in range(1, nd)]
    g_ret[me_d] = g_send[me_d]
    own_grad = mm_nt(grad_pre, w_self[...]) + to_tiles(0, own_tiles, grad_num)

    for copy in w2:
        copy.wait_recv()
    total = w2_recv[0].astype(F32)
    for i in range(1, ny):
        total = total + w2_recv[i].astype(F32)
    w3_send[...] = total
    w3 = [
        push(w3_send.at[x_at(j)], w3_recv.at[x], w3_s.at[j], w3_r.at[j], me_d, z * nx + x_at(j)) for j in range(1, nx)]
    w3_recv[x] = w3_send[x]

    for copy in hub_gx:
        copy.wait_recv()
    total = h_recv[0].astype(F32)
    for j in range(1, nx):
        total = total + h_recv[j].astype(F32)
    h2_send[...] = total.astype(BF16)
    hub_gz = [
        push(h2_send.at[z_at(k)], h2_recv.at[z], gz_s.at[k], gz_r.at[k], me_d, z_at(k) * nx + x) for k in range(1, nz)]
    h2_recv[z] = h2_send[z]

    for copy in w3:
        copy.wait_recv()
    total = w3_recv[0]
    for j in range(1, nx):
        total = total + w3_recv[j]
    w4_recv[z] = total.astype(BF16)
    w4 = [
        push(w4_recv.at[z], w4_recv.at[z], w4_s.at[k], w4_r.at[k], me_d, z_at(k) * nx + x) for k in range(1, nz)]

    for copy in ret:
        copy.wait_recv()
    own_grad = own_grad + mm(pick_t[...], g_ret[...].reshape(nd * slots, width))

    for copy in w4:
        copy.wait_recv()
    total = w4_recv[0].astype(F32)
    for k in range(1, nz):
        total = total + w4_recv[k].astype(F32)
    w_fin[core, x, y] = total.astype(BF16)
    w5 = [
        push(w_fin.at[core, x, y], w_fin.at[core, x, y], w5_s.at[k], w5_r.at[k], y_at(k) * CORES + core, me_g)
        for k in range(1, ny)]

    for copy in hub_gz:
        copy.wait_recv()
    hub_total = h2_recv[0].astype(F32)
    for k in range(1, nz):
        hub_total = hub_total + h2_recv[k].astype(F32)
    hub_pick_t = jnp.where(
        lax.broadcasted_iota(jnp.int32, (nodes, hubs), 0).astype(F32) == jnp.broadcast_to(hub_index, (nodes, hubs)),
        1.0, 0.0).astype(BF16)
    high = hub_total.astype(BF16)
    low = (hub_total - high.astype(F32)).astype(BF16)
    grad_feat[...] = (own_grad + mm(hub_pick_t, high) + mm(hub_pick_t, low)).astype(BF16)

    for copy in w5:
        copy.wait_recv()
    w6 = [
        push(w_fin.at[core, x], w_fin.at[core, x], w6_s.at[j], w6_r.at[j], me_d, z * nx + x_at(j))
        for j in range(1, nx)]
    w7 = [push(w_fin.at[core, x], w_fin.at[core, x], w7_s.at[0], w7_r.at[0], sibling, me_g)]
    for j in range(1, nx):
        w6[j - 1].wait_recv()
        from_x = lax.rem(x + nx - j, nx)
        w7.append(push(w_fin.at[core, from_x], w_fin.at[core, from_x], w7_s.at[j], w7_r.at[j], sibling, me_g))
    for copy in w7:
        copy.wait_recv()
    for matrix, result in enumerate((grad_self, grad_neigh)):
        for j in range(nx):
            for i in range(ny):
                top = i * yrows + (j // 2) * crows
                result[top:top + crows, (j % 2) * 128:(j % 2) * 128 + 128] = w_fin[matrix, j, i].astype(F32)

    for copy in pending:
        copy.wait_send()


def on_device(dims, features, w_self, w_neigh, adjacency, tile_ids, send_rows, send_counts, hub_rows, cotangent):
    nd, ny, nz, nx = dims
    nodes, width = features.shape
    row_tiles, _, tile, _ = adjacency.shape
    slots, hubs = send_rows.shape[1], hub_rows.shape[1]
    src_tiles = (nodes + nd * slots + nz * nx * hubs) // tile
    crows = nodes // ny // (nx // 2)
    vmem = pl.BlockSpec(memory_space=pltpu.VMEM)
    smem = pl.BlockSpec(memory_space=pltpu.SMEM)
    dma = pltpu.SemaphoreType.DMA
    pairs = [(nd,), (nz,), (nx, nz), (nd,), (nx,), (nz,), (), (ny,), (nx,), (nz,), (ny,), (nx,), (nx,)]
    return pl.pallas_call(
        functools.partial(kernel, dims),
        out_shape=(
            jax.ShapeDtypeStruct((nodes, width), BF16),
            jax.ShapeDtypeStruct((nodes, width), BF16),
            jax.ShapeDtypeStruct((width, width), F32),
            jax.ShapeDtypeStruct((width, width), F32),
        ),
        in_specs=[vmem, vmem, vmem, vmem, smem, vmem, vmem, vmem, vmem],
        out_specs=[vmem] * 4,
        scratch_shapes=[
            pltpu.VMEM((nd, slots, width), BF16),
            pltpu.VMEM((nd, slots, width), BF16),
            pltpu.VMEM((nz, nx, hubs, width), BF16),
            pltpu.VMEM((src_tiles, nodes, tile), BF16),
            pltpu.VMEM((src_tiles, tile, nodes), BF16),
            pltpu.VMEM((src_tiles, nodes, tile), BF16),
            pltpu.VMEM((src_tiles, tile, nodes), BF16),
            pltpu.VMEM((nd * slots, nodes), BF16),
            pltpu.VMEM((nodes, nd * slots), BF16),
            pltpu.VMEM((width, nodes), BF16),
            pltpu.VMEM((nd, slots, width), BF16),
            pltpu.VMEM((nd, slots, width), BF16),
            pltpu.VMEM((nx, nz, hubs, width), BF16),
            pltpu.VMEM((nx, nz, hubs, width), BF16),
            pltpu.VMEM((nz, hubs, width), BF16),
            pltpu.VMEM((nz, hubs, width), BF16),
            pltpu.VMEM((2, width, width), F32),
            pltpu.VMEM((width, width), F32),
            pltpu.VMEM((ny, nx, crows, 128), BF16),
            pltpu.VMEM((ny, nx, crows, 128), BF16),
            pltpu.VMEM((nx, crows, 128), F32),
            pltpu.VMEM((nx, crows, 128), F32),
            pltpu.VMEM((nz, crows, 128), BF16),
            pltpu.VMEM((2, nx, ny, crows, 128), BF16),
        ] + [dma(shape) for shape in pairs for _ in range(2)],
        compiler_params=pltpu.CompilerParams(
            collective_id=0, has_side_effects=True, vmem_limit_bytes=40 * 1024 * 1024),
    )(features, w_self, w_neigh, adjacency, tile_ids, send_rows, send_counts, hub_rows, cotangent)


def solution(mesh):
    nd, ng = mesh.shape["dom"], mesh.shape["grp"]
    dims = (nd, nd // CORES, ng // X_CHIPS, X_CHIPS)
    placed = (
        P(("dom", "grp"), None),
        P(),
        P(),
        P(("dom", "grp"), None, None, None),
        P(("dom", "grp"), None),
        P(("dom", "grp"), None),
        P(("dom", "grp"), None),
        P(("dom", "grp"), None),
        P(("dom", "grp"), None),
    )
    return jax.shard_map(
        functools.partial(on_device, dims),
        mesh=mesh,
        in_specs=placed,
        out_specs=(P(("dom", "grp"), None), P(("dom", "grp"), None), P(), P()),
        check_vma=False,
    )
```

```python
import functools

import jax
import jax.numpy as jnp
from jax import lax
from jax.experimental import pallas as pl
from jax.experimental.pallas import tpu as pltpu
from jax.sharding import PartitionSpec as P

CORES = 2
X_CHIPS = 4

VMEM_LIMIT = 60 * 1024 * 1024

F32 = jnp.float32
BF16 = jnp.bfloat16


def mm(a, b):
    return jnp.dot(a, b, preferred_element_type=F32)


def mm_nt(a, b):
    return lax.dot_general(a, b, (((1,), (1,)), ((), ())), preferred_element_type=F32)


def far_first(*sizes):
    offsets = [()]
    for size in sizes:
        offsets = [o + (k,) for o in offsets for k in range(size)]
    hops = lambda o: sum(min(k, size - k) for k, size in zip(o, sizes))
    return sorted((o for o in offsets if any(o)), key=lambda o: -hops(o))


def kernel(
    dims,
    feat_in, w_self_in, w_neigh_in, adj_in, ids_in, send_rows_in, send_counts_in, hub_rows_in, cot_in,
    out_to, grad_feat_to, w_fin_to,
    feat, w_self, w_neigh, adj, ids, send_rows, send_counts, hub_rows, cot, load_sem,
    out, grad_feat, store_sem,
    out_send, halo_in, hub_in, dense, dense_t, dense_low, dense_low_t, pick, pick_t, lhs_t,
    g_send, g_ret, h_send, h_recv, h2_send, h2_recv,
    gw, w_sib, w2_send, w2_recv, w4_recv, w_fin,
    halo_s, halo_r, hz_s, hz_r, hx_s, hx_r, gh_s, gh_r, gx_s, gx_r, gz_s, gz_r,
    w1_s, w1_r, w2_s, w2_r, w4_s, w4_r, w5_s, w5_r, w7_s, w7_r,
):
    nd, ny, nz, nx = dims
    nodes, width = feat.shape
    row_tiles, per_row, tile, _ = adj.shape
    slots = send_rows.shape[1]
    hubs = hub_rows.shape[1]
    src_tiles = dense.shape[0]
    own_tiles = nodes // tile
    halo_tiles = nd * slots // tile
    crows = w_fin.shape[3]
    me_d = lax.axis_index("dom")
    me_g = lax.axis_index("grp")
    y, core = lax.div(me_d, CORES), lax.rem(me_d, CORES)
    z, x = lax.div(me_g, nx), lax.rem(me_g, nx)

    def dom_at(k):
        return lax.rem(me_d + k, nd)

    def z_at(k):
        return lax.rem(z + k, nz)

    def x_at(k):
        return lax.rem(x + k, nx)

    def y_at(k):
        return lax.rem(y + k, ny)

    sibling = y * CORES + (1 - core)
    pending = []

    def push(src, dst, send_sem, recv_sem, d, g):
        copy = pltpu.make_async_remote_copy(
            src_ref=src, dst_ref=dst, send_sem=send_sem, recv_sem=recv_sem,
            device_id=(d, g), device_id_type=pl.DeviceIdType.MESH,
        )
        copy.start()
        pending.append(copy)
        return copy

    def arrive(*copies):
        for copy in copies:
            copy.wait_recv()

    loads = [
        pltpu.make_async_copy(src, dst, load_sem.at[i])
        for i, (src, dst) in enumerate((
            (hub_rows_in, hub_rows), (feat_in, feat), (send_counts_in, send_counts), (send_rows_in, send_rows),
            (ids_in, ids), (adj_in, adj), (w_self_in, w_self), (w_neigh_in, w_neigh), (cot_in, cot)))
    ]
    for load in loads:
        load.start()

    barrier = pltpu.get_barrier_semaphore()
    partners = [(dom_at(k), me_g) for k in range(1, nd)]
    partners += [(me_d, z_at(k) * nx + x) for k in range(1, nz)]
    partners += [(me_d, z * nx + x_at(k)) for k in range(1, nx)]
    for partner in partners:
        pl.semaphore_signal(barrier, inc=1, device_id=partner, device_id_type=pl.DeviceIdType.MESH)

    far = max(1, nz // 3)
    far_z = [k for (k,) in far_first(nz)]
    far_x = [k for (k,) in far_first(nx)]
    own_slot = nz - far
    for load in loads[:2]:
        load.wait()
    features = feat[...]
    hub_index = hub_rows[...].astype(F32)
    hub_eye = lax.broadcasted_iota(jnp.int32, (hubs, hubs), 0) == lax.broadcasted_iota(jnp.int32, (hubs, hubs), 1)
    hub_col = jnp.sum(
        jnp.where(hub_eye, jnp.broadcast_to(hub_index, (hubs, hubs)), 0.0), axis=1, keepdims=True)
    hub_pick = jnp.where(
        lax.broadcasted_iota(jnp.int32, (hubs, nodes), 1).astype(F32) == hub_col, 1.0, 0.0).astype(BF16)
    hub_in[x, own_slot] = mm(hub_pick, features).astype(BF16)

    pl.semaphore_wait(barrier, len(partners))

    hub_z = {}
    for k in far_z:
        hub_z[k] = push(
            hub_in.at[x, own_slot], hub_in.at[x, (k - far) % nz], hz_s.at[k], hz_r.at[k], me_d, z_at(k) * nx + x)
    hub_x = []

    def forward(group, first, last):
        block = hub_in.at[x, pl.ds(first, last - first)]
        for j in far_x:
            hub_x.append(push(block, block, hx_s.at[j, group], hx_r.at[j, group], me_d, z * nx + x_at(j)))

    forward(0, own_slot, own_slot + 1)

    for load in loads[2:4]:
        load.wait()
    count_col = jnp.sum(
        jnp.where(
            lax.broadcasted_iota(jnp.int32, (nd, nd), 0) == lax.broadcasted_iota(jnp.int32, (nd, nd), 1),
            jnp.broadcast_to(send_counts[...], (nd, nd)), 0).astype(F32),
        axis=1, keepdims=True)
    live = lax.broadcasted_iota(jnp.int32, (nd, slots), 1).astype(F32) < count_col
    index = jnp.where(live, send_rows[...].astype(F32), -1.0)
    eye = lax.broadcasted_iota(jnp.int32, (slots, slots), 0) == lax.broadcasted_iota(jnp.int32, (slots, slots), 1)
    lane = lax.broadcasted_iota(jnp.int32, (slots, nodes), 1).astype(F32)
    for p in range(nd):
        column = jnp.sum(
            jnp.where(eye, jnp.broadcast_to(index[p:p + 1, :], (slots, slots)), 0.0), axis=1, keepdims=True)
        pick[p * slots:(p + 1) * slots, :] = jnp.where(lane == column, 1.0, 0.0).astype(BF16)
    out_send[...] = mm(pick[...], features).astype(BF16).reshape(nd, slots, width)
    halo_in[me_d] = out_send[me_d]
    far_dom = [i * CORES + j for i, j in far_first(ny, CORES)]
    halo = [
        push(out_send.at[dom_at(k)], halo_in.at[me_d], halo_s.at[k], halo_r.at[k], dom_at(k), me_g) for k in far_dom]

    def gather_tiles(c, carry):
        parts = []
        for r in range(row_tiles):
            total = jnp.zeros((tile, tile), F32)
            for t in range(per_row):
                total = total + jnp.where(ids[r, t] == c, adj[r, t].astype(F32), 0.0)
            parts.append(total)
        block = jnp.concatenate(parts, axis=0)
        high = block.astype(BF16)
        low = block - high.astype(F32)
        dense[c] = high
        dense_low[c] = low.astype(BF16)
        dense_t[c] = high.astype(F32).T.astype(BF16)
        dense_low_t[c] = low.T.astype(BF16)
        return carry

    for load in loads[4:]:
        load.wait()
    lax.fori_loop(0, src_tiles, gather_tiles, 0)

    arrive(*[hub_z[k] for k in range(far, nz - far + 1)])
    forward(1, 0, nz - 2 * far + 1)
    arrive(*[hub_z[k] for k in far_z if not far <= k <= nz - far])
    if far > 1:
        forward(2, nz - 2 * far + 1, own_slot)
        forward(3, own_slot + 1, nz)

    sums = []
    for r in range(row_tiles):
        total = jnp.zeros((tile, tile), F32)
        for t in range(per_row):
            total = total + adj[r, t].astype(F32)
        sums.append(jnp.sum(total, axis=1, keepdims=True))
    inverse = 1.0 / (1.0 + jnp.concatenate(sums, axis=0))
    lhs_t[0] = features.astype(F32).T.astype(BF16)
    pick_t[...] = pick[...].astype(F32).T.astype(BF16)

    def from_tiles(first, count, rows):
        return sum(
            mm(jnp.concatenate([part[c] for c in range(first, first + count)], axis=1), rows)
            for part in (dense, dense_low))

    def to_tiles(first, count, rows):
        return sum(
            mm(part[first:first + count].reshape(count * tile, nodes), rows) for part in (dense_t, dense_low_t))

    numer = from_tiles(0, own_tiles, features)
    pre = mm(features, w_self[...])
    arrive(*halo)
    numer = numer + from_tiles(own_tiles, halo_tiles, halo_in[...].reshape(nd * slots, width))
    arrive(*hub_x)
    hub_rows_all = jnp.concatenate(
        [hub_in[j, lax.rem(z - i - far + 2 * nz, nz)] for i in range(nz) for j in range(nx)], axis=0)
    hub_tiles = src_tiles - own_tiles - halo_tiles
    numer = numer + from_tiles(own_tiles + halo_tiles, hub_tiles, hub_rows_all)
    agg = numer * inverse
    agg_b = agg.astype(BF16)
    pre = pre + mm(agg_b, w_neigh[...])
    sig = 1.0 / (1.0 + jnp.exp(-pre))
    out[...] = (pre * sig).astype(BF16)
    stores = [pltpu.make_async_copy(out, out_to, store_sem.at[0])]
    stores[-1].start()
    grad_pre = (cot[...].astype(F32) * sig * (1.0 + pre * (1.0 - sig))).astype(BF16)

    lhs_t[1] = agg_b.astype(F32).T.astype(BF16)
    gw[...] = mm(lhs_t[1 - core], grad_pre)
    w1 = push(gw, w_sib, w1_s, w1_r, sibling, me_g)
    mine = mm(lhs_t[core], grad_pre)

    grad_num = (mm_nt(grad_pre, w_neigh[...]) * inverse).astype(BF16)
    hub_grad = to_tiles(own_tiles + halo_tiles, hub_tiles, grad_num).astype(BF16)
    for g in range(nz * nx):
        h_send[g % nx, g // nx] = hub_grad[g * hubs:(g + 1) * hubs, :]
    g_send[...] = to_tiles(own_tiles, halo_tiles, grad_num).astype(BF16).reshape(nd, slots, width)

    arrive(w1)
    mine = mine + w_sib[...]
    yrows = nodes // ny
    plane = far_first(ny, nx)
    for i in range(ny):
        for j in range(nx):
            top = i * yrows + (j // 2) * crows
            w2_send[i, j] = mine[top:top + crows, (j % 2) * 128:(j % 2) * 128 + 128].astype(BF16)
    w2 = [
        push(w2_send.at[y_at(i), x_at(j)], w2_recv.at[n + 1], w2_s.at[n], w2_r.at[n], y_at(i) * CORES + core,
             z * nx + x_at(j)) for n, (i, j) in enumerate(plane)]
    w2_recv[0] = w2_send[y, x]
    hub_gx = [
        push(h_send.at[x_at(j)], h_recv.at[x], gx_s.at[j], gx_r.at[j], me_d, z * nx + x_at(j)) for j in far_x]
    h_recv[x] = h_send[x]
    own_grad = mm_nt(grad_pre, w_self[...]) + to_tiles(0, own_tiles, grad_num)

    arrive(*w2)
    w4_recv[z] = jnp.sum(w2_recv[...].astype(F32), axis=0).astype(BF16)
    w4 = [
        push(w4_recv.at[z], w4_recv.at[z], w4_s.at[k], w4_r.at[k], me_d, z_at(k) * nx + x) for k in far_z]
    ret = [
        push(g_send.at[dom_at(k)], g_ret.at[me_d], gh_s.at[k], gh_r.at[k], dom_at(k), me_g) for k in far_dom]
    g_ret[me_d] = g_send[me_d]

    arrive(*hub_gx)
    h2_send[...] = jnp.sum(h_recv[...].astype(F32), axis=0).astype(BF16)

    arrive(*w4)
    w_fin[core, x, y] = jnp.sum(w4_recv[...].astype(F32), axis=0).astype(BF16)
    w5 = [
        push(w_fin.at[core, x, y], w_fin.at[core, x, y], w5_s.at[n], w5_r.at[n], y_at(i) * CORES + core,
             z * nx + x_at(j)) for n, (i, j) in enumerate(plane)]
    hub_gz = [
        push(h2_send.at[z_at(k)], h2_recv.at[z], gz_s.at[k], gz_r.at[k], me_d, z_at(k) * nx + x) for k in far_z]
    h2_recv[z] = h2_send[z]

    arrive(*ret)
    own_grad = own_grad + mm(pick_t[...], g_ret[...].reshape(nd * slots, width))

    arrive(*w5)
    w7 = push(w_fin.at[core], w_fin.at[core], w7_s, w7_r, sibling, me_g)

    arrive(*hub_gz)
    hub_total = jnp.sum(h2_recv[...].astype(F32), axis=0)
    hub_pick_t = jnp.where(
        lax.broadcasted_iota(jnp.int32, (nodes, hubs), 0).astype(F32) == jnp.broadcast_to(hub_index, (nodes, hubs)),
        1.0, 0.0).astype(BF16)
    high = hub_total.astype(BF16)
    low = (hub_total - high.astype(F32)).astype(BF16)
    grad_feat[...] = (own_grad + mm(hub_pick_t, high) + mm(hub_pick_t, low)).astype(BF16)
    stores.append(pltpu.make_async_copy(grad_feat, grad_feat_to, store_sem.at[1]))
    stores[-1].start()

    arrive(w7)
    stores.append(pltpu.make_async_copy(w_fin, w_fin_to, store_sem.at[2]))
    stores[-1].start()
    for copy in pending:
        copy.wait_send()
    for copy in stores:
        copy.wait()


def store(out_in, grad_in, w_in, out_to, grad_to, self_to, neigh_to, out, grad, w_fin, grad_self, grad_neigh, load_sem, store_sem):
    loads = [
        pltpu.make_async_copy(src, via, load_sem.at[i])
        for i, (src, via) in enumerate(((w_in, w_fin), (out_in, out), (grad_in, grad)))]
    stores = [
        pltpu.make_async_copy(via, dst, store_sem.at[i])
        for i, (via, dst) in enumerate(((grad_self, self_to), (grad_neigh, neigh_to), (out, out_to), (grad, grad_to)))]
    for load in loads:
        load.start()
    for load in loads:
        load.wait()
    stores[2].start()
    stores[3].start()
    _, nx, ny, crows, _ = w_fin.shape
    for matrix, result in enumerate((grad_self, grad_neigh)):
        for j in range(nx):
            for i in range(ny):
                top = (i * (nx // 2) + j // 2) * crows
                result[top:top + crows, (j % 2) * 128:(j % 2) * 128 + 128] = w_fin[matrix, j, i].astype(F32)
        stores[matrix].start()
    for copy in stores:
        copy.wait()


def on_device(dims, features, w_self, w_neigh, adjacency, tile_ids, send_rows, send_counts, hub_rows, cotangent):
    nd, ny, nz, nx = dims
    nodes, width = features.shape
    row_tiles, _, tile, _ = adjacency.shape
    slots, hubs = send_rows.shape[1], hub_rows.shape[1]
    src_tiles = (nodes + nd * slots + nz * nx * hubs) // tile
    crows = nodes // ny // (nx // 2)
    args = (features, w_self, w_neigh, adjacency, tile_ids, send_rows, send_counts, hub_rows, cotangent)
    hbm = pl.BlockSpec(memory_space=pltpu.HBM)
    dma = pltpu.SemaphoreType.DMA
    pairs = [(nd,), (nz,), (nx, 4), (nd,), (nx,), (nz,), (), (ny * nx,), (nz,), (ny * nx,), ()]
    results = pl.pallas_call(
        functools.partial(kernel, dims),
        out_shape=(
            jax.ShapeDtypeStruct((nodes, width), BF16),
            jax.ShapeDtypeStruct((nodes, width), BF16),
            jax.ShapeDtypeStruct((2, nx, ny, crows, 128), BF16),
        ),
        in_specs=[hbm] * len(args),
        out_specs=[hbm] * 3,
        scratch_shapes=[
            (pltpu.SMEM if arg is tile_ids else pltpu.VMEM)(arg.shape, arg.dtype) for arg in args
        ] + [
            dma((len(args),)),
            pltpu.VMEM((nodes, width), BF16),
            pltpu.VMEM((nodes, width), BF16),
            dma((3,)),
            pltpu.VMEM((nd, slots, width), BF16),
            pltpu.VMEM((nd, slots, width), BF16),
            pltpu.VMEM((nx, nz, hubs, width), BF16),
            pltpu.VMEM((src_tiles, nodes, tile), BF16),
            pltpu.VMEM((src_tiles, tile, nodes), BF16),
            pltpu.VMEM((src_tiles, nodes, tile), BF16),
            pltpu.VMEM((src_tiles, tile, nodes), BF16),
            pltpu.VMEM((nd * slots, nodes), BF16),
            pltpu.VMEM((nodes, nd * slots), BF16),
            pltpu.VMEM((2, width, nodes), BF16),
            pltpu.VMEM((nd, slots, width), BF16),
            pltpu.VMEM((nd, slots, width), BF16),
            pltpu.VMEM((nx, nz, hubs, width), BF16),
            pltpu.VMEM((nx, nz, hubs, width), BF16),
            pltpu.VMEM((nz, hubs, width), BF16),
            pltpu.VMEM((nz, hubs, width), BF16),
            pltpu.VMEM((width, width), F32),
            pltpu.VMEM((width, width), F32),
            pltpu.VMEM((ny, nx, crows, 128), BF16),
            pltpu.VMEM((ny * nx, crows, 128), BF16),
            pltpu.VMEM((nz, crows, 128), BF16),
            pltpu.VMEM((2, nx, ny, crows, 128), BF16),
        ] + [dma(shape) for shape in pairs for _ in range(2)],
        compiler_params=pltpu.CompilerParams(
            collective_id=0, has_side_effects=True, vmem_limit_bytes=VMEM_LIMIT),
    )(*args)
    rows = jax.ShapeDtypeStruct((nodes, width), BF16)
    weights = jax.ShapeDtypeStruct((width, width), F32)
    return pl.pallas_call(
        store,
        out_shape=(rows, rows, weights, weights),
        in_specs=[hbm] * 3,
        out_specs=[hbm] * 4,
        scratch_shapes=[pltpu.VMEM(r.shape, r.dtype) for r in (*results, weights, weights)] + [dma((3,)), dma((4,))],
        compiler_params=pltpu.CompilerParams(vmem_limit_bytes=VMEM_LIMIT),
    )(*results)


def solution(mesh):
    nd, ng = mesh.shape["dom"], mesh.shape["grp"]
    dims = (nd, nd // CORES, ng // X_CHIPS, X_CHIPS)
    placed = (
        P(("dom", "grp"), None),
        P(),
        P(),
        P(("dom", "grp"), None, None, None),
        P(("dom", "grp"), None),
        P(("dom", "grp"), None),
        P(("dom", "grp"), None),
        P(("dom", "grp"), None),
        P(("dom", "grp"), None),
    )
    return jax.shard_map(
        functools.partial(on_device, dims),
        mesh=mesh,
        in_specs=placed,
        out_specs=(P(("dom", "grp"), None), P(("dom", "grp"), None), P(), P()),
        check_vma=False,
    )
```

```python
import functools

import jax
import jax.numpy as jnp
from jax import lax
from jax.experimental import pallas as pl
from jax.experimental.pallas import tpu as pltpu
from jax.sharding import PartitionSpec as P

CORES = 2
X_CHIPS = 4

VMEM_LIMIT = 60 * 1024 * 1024

F32 = jnp.float32
BF16 = jnp.bfloat16


def mm(a, b):
    return jnp.dot(a, b, preferred_element_type=F32)


def mm_nt(a, b):
    return lax.dot_general(a, b, (((1,), (1,)), ((), ())), preferred_element_type=F32)


def far_first(*sizes):
    offsets = [()]
    for size in sizes:
        offsets = [o + (k,) for o in offsets for k in range(size)]
    hops = lambda o: sum(min(k, size - k) for k, size in zip(o, sizes))
    return sorted((o for o in offsets if any(o)), key=lambda o: -hops(o))


def kernel(
    dims,
    feat_in, w_self_in, w_neigh_in, adj_in, ids_in, send_rows_in, send_counts_in, hub_rows_in, cot_in,
    out_to, grad_feat_to, w_fin_to,
    feat, w_self, w_neigh, adj, ids, send_rows, send_counts, hub_rows, cot, load_sem,
    out, grad_feat, store_sem,
    out_send, halo_in, hub_own, hub_in, dense, dense_t, dense_low, dense_low_t, pick, pick_t, lhs_t,
    g_send, g_ret, h_send, h_recv, h2_send, h2_recv,
    gw, w_sib, w2_send, w2_recv, w4_recv, w_fin,
    halo_s, halo_r, hz_s, hz_r, hx_s, hx_r, gh_s, gh_r, gx_s, gx_r, gz_s, gz_r,
    w1_s, w1_r, w2_s, w2_r, w4_s, w4_r, w5_s, w5_r, w7_s, w7_r,
):
    nd, ny, nz, nx = dims
    nodes, width = feat.shape
    row_tiles, per_row, tile, _ = adj.shape
    slots = send_rows.shape[1]
    hubs = hub_rows.shape[1]
    src_tiles = dense.shape[0]
    own_tiles = nodes // tile
    halo_tiles = nd * slots // tile
    crows = w_fin.shape[2]
    me_d = lax.axis_index("dom")
    me_g = lax.axis_index("grp")
    y, core = lax.div(me_d, CORES), lax.rem(me_d, CORES)
    z, x = lax.div(me_g, nx), lax.rem(me_g, nx)

    def dom_at(k):
        return lax.rem(me_d + k, nd)

    def z_at(k):
        return lax.rem(z + k, nz)

    def x_at(k):
        return lax.rem(x + k, nx)

    def y_at(k):
        return lax.rem(y + k, ny)

    sibling = y * CORES + (1 - core)
    def copy_of(src, dst, send_sem, recv_sem, d, g):
        return pltpu.make_async_remote_copy(
            src_ref=src, dst_ref=dst, send_sem=send_sem, recv_sem=recv_sem,
            device_id=(d, g), device_id_type=pl.DeviceIdType.MESH,
        )

    def push(*copy):
        copy_of(*copy).start()

    def arrive(size, send_sem, recv_sem):
        copy_of(size, size, send_sem, recv_sem, sibling, me_g).wait_recv()

    def sent(size, send_sem, recv_sem):
        copy_of(size, size, send_sem, recv_sem, sibling, me_g).wait_send()

    loads = [
        pltpu.make_async_copy(src, dst, load_sem.at[i])
        for i, (src, dst) in enumerate((
            (hub_rows_in, hub_rows), (feat_in, feat), (send_counts_in, send_counts), (send_rows_in, send_rows),
            (ids_in, ids), (adj_in, adj), (w_self_in, w_self), (w_neigh_in, w_neigh), (cot_in, cot)))
    ]
    for load in loads:
        load.start()

    barrier = pltpu.get_barrier_semaphore()
    far_z = [k for (k,) in far_first(nz)]
    far_x = [k for (k,) in far_first(nx)]
    far_dom = [i * CORES + j for i, j in far_first(ny, CORES)]
    partners = [(me_d, z_at(k) * nx + x) for k in far_z]
    partners += [(me_d, z * nx + x_at(k)) for k in far_x]
    partners += [(dom_at(k), me_g) for k in far_dom]
    for partner in partners:
        pl.semaphore_signal(barrier, inc=1, device_id=partner, device_id_type=pl.DeviceIdType.MESH)

    z_group = nz // 4
    for load in loads[:2]:
        load.wait()
    features = feat[...]
    hub_index = hub_rows[...].astype(F32)
    hub_eye = lax.broadcasted_iota(jnp.int32, (hubs, hubs), 0) == lax.broadcasted_iota(jnp.int32, (hubs, hubs), 1)
    hub_col = jnp.sum(
        jnp.where(hub_eye, jnp.broadcast_to(hub_index, (hubs, hubs)), 0.0), axis=1, keepdims=True)
    hub_pick = jnp.where(
        lax.broadcasted_iota(jnp.int32, (hubs, nodes), 1).astype(F32) == hub_col, 1.0, 0.0).astype(BF16)
    hub_own[...] = mm(hub_pick, features).astype(BF16)

    for load in loads[2:4]:
        load.wait()
    count_col = jnp.sum(
        jnp.where(
            lax.broadcasted_iota(jnp.int32, (nd, nd), 0) == lax.broadcasted_iota(jnp.int32, (nd, nd), 1),
            jnp.broadcast_to(send_counts[...], (nd, nd)), 0).astype(F32),
        axis=1, keepdims=True)
    live = lax.broadcasted_iota(jnp.int32, (nd, slots), 1).astype(F32) < count_col
    index = jnp.where(live, send_rows[...].astype(F32), -1.0)
    total_slots = nd * slots
    slot = lax.broadcasted_iota(jnp.int32, (total_slots, slots), 0)
    own_part = lax.div(lax.broadcasted_iota(jnp.int32, (total_slots, nd), 0), slots) == lax.broadcasted_iota(
        jnp.int32, (total_slots, nd), 1)
    spread = mm(jnp.where(own_part, 1.0, 0.0).astype(BF16), index.astype(BF16))
    spread = jnp.where(lax.rem(slot, slots) == lax.broadcasted_iota(jnp.int32, (total_slots, slots), 1), spread, 0.0)
    spread = mm(spread.astype(BF16), jnp.ones((slots, nodes), BF16))
    lane = lax.broadcasted_iota(jnp.int32, (total_slots, nodes), 1).astype(F32)
    pick[...] = jnp.where(lane == spread, 1.0, 0.0).astype(BF16)
    out_send[...] = mm(pick[...], features).astype(BF16).reshape(nd, slots, width)
    halo_in[me_d] = out_send[me_d]
    pl.semaphore_wait(barrier, len(partners))

    for k in far_z:
        push(hub_own, hub_in.at[x, z], hz_s, hz_r.at[lax.div(z, z_group)], me_d, z_at(k) * nx + x)
    pltpu.make_async_copy(hub_own, hub_in.at[x, z], hz_r.at[lax.div(z, z_group)]).start()
    for k in far_dom:
        push(out_send.at[dom_at(k)], halo_in.at[me_d], halo_s, halo_r, dom_at(k), me_g)

    def gather_tiles(c, carry):
        parts = []
        for r in range(row_tiles):
            total = jnp.zeros((tile, tile), F32)
            for t in range(per_row):
                total = total + jnp.where(ids[r, t] == c, adj[r, t].astype(F32), 0.0)
            parts.append(total)
        block = jnp.concatenate(parts, axis=0)
        high = block.astype(BF16)
        low = block - high.astype(F32)
        dense[c] = high
        dense_low[c] = low.astype(BF16)
        dense_t[c] = high.astype(F32).T.astype(BF16)
        dense_low_t[c] = low.T.astype(BF16)
        return carry

    for load in loads[4:]:
        load.wait()
    lax.fori_loop(0, src_tiles, gather_tiles, 0)

    for group in range(4):
        block = hub_in.at[x, pl.ds(group * z_group, z_group)]
        arrive(block, hz_s, hz_r.at[group])
        for j in far_x:
            push(block, block, hx_s, hx_r, me_d, z * nx + x_at(j))

    sums = []
    for r in range(row_tiles):
        total = jnp.zeros((tile, tile), F32)
        for t in range(per_row):
            total = total + adj[r, t].astype(F32)
        sums.append(jnp.sum(total, axis=1, keepdims=True))
    inverse = 1.0 / (1.0 + jnp.concatenate(sums, axis=0))
    lhs_t[0] = features.astype(F32).T.astype(BF16)
    pick_t[...] = pick[...].astype(F32).T.astype(BF16)

    def from_tiles(first, count, rows):
        return sum(
            mm(jnp.concatenate([part[c] for c in range(first, first + count)], axis=1), rows)
            for part in (dense, dense_low))

    def to_tiles(first, count, rows):
        return sum(
            mm(part[first:first + count].reshape(count * tile, nodes), rows) for part in (dense_t, dense_low_t))

    numer = from_tiles(0, own_tiles, features)
    pre = mm(features, w_self[...])
    arrive(halo_in.at[pl.ds(0, nd - 1)], halo_s, halo_r)
    numer = numer + from_tiles(own_tiles, halo_tiles, halo_in[...].reshape(nd * slots, width))
    arrive(hub_in.at[pl.ds(0, nx - 1)], hx_s, hx_r)
    hub_rows_all = jnp.concatenate(
        [hub_in[j, i] for i in range(nz) for j in range(nx)], axis=0)
    hub_tiles = src_tiles - own_tiles - halo_tiles
    numer = numer + from_tiles(own_tiles + halo_tiles, hub_tiles, hub_rows_all)
    agg = numer * inverse
    agg_b = agg.astype(BF16)
    pre = pre + mm(agg_b, w_neigh[...])
    sig = 1.0 / (1.0 + jnp.exp(-pre))
    out[...] = (pre * sig).astype(BF16)
    stores = [pltpu.make_async_copy(out, out_to, store_sem.at[0])]
    stores[-1].start()
    grad_pre = (cot[...].astype(F32) * sig * (1.0 + pre * (1.0 - sig))).astype(BF16)

    lhs_t[1] = agg_b.astype(F32).T.astype(BF16)
    gw[...] = mm(lhs_t[1 - core], grad_pre)
    push(gw, w_sib, w1_s, w1_r, sibling, me_g)
    mine = mm(lhs_t[core], grad_pre)

    grad_num = (mm_nt(grad_pre, w_neigh[...]) * inverse).astype(BF16)
    hub_grad = to_tiles(own_tiles + halo_tiles, hub_tiles, grad_num).astype(BF16)
    for g in range(nz * nx):
        h_send[g % nx, g // nx] = hub_grad[g * hubs:(g + 1) * hubs, :]
    for j in far_x:
        push(h_send.at[x_at(j)], h_recv.at[x], gx_s, gx_r, me_d, z * nx + x_at(j))
    h_recv[x] = h_send[x]
    g_send[...] = to_tiles(own_tiles, halo_tiles, grad_num).astype(BF16).reshape(nd, slots, width)

    arrive(w_sib, w1_s, w1_r)
    mine = mine + w_sib[...]
    yrows = nodes // ny
    plane = far_first(ny, nx)
    for i in range(ny):
        for j in range(nx):
            top = i * yrows + (j // 2) * crows
            w2_send[i * nx + j] = mine[top:top + crows, (j % 2) * 128:(j % 2) * 128 + 128].astype(BF16)
    for n, (i, j) in enumerate(plane):
        push(w2_send.at[y_at(i) * nx + x_at(j)], w2_recv.at[n + 1], w2_s, w2_r, y_at(i) * CORES + core,
             z * nx + x_at(j))
    w2_recv[0] = w2_send[y * nx + x]
    own_grad = mm_nt(grad_pre, w_self[...]) + to_tiles(0, own_tiles, grad_num)

    arrive(w2_recv.at[pl.ds(1, len(plane))], w2_s, w2_r)
    w4_recv[z] = jnp.sum(w2_recv[...].astype(F32), axis=0).astype(BF16)
    for k in far_z:
        push(w4_recv.at[z], w4_recv.at[z], w4_s, w4_r, me_d, z_at(k) * nx + x)
    for k in far_dom:
        push(g_send.at[dom_at(k)], g_ret.at[me_d], gh_s, gh_r, dom_at(k), me_g)
    g_ret[me_d] = g_send[me_d]

    arrive(h_recv.at[pl.ds(0, nx - 1)], gx_s, gx_r)
    h2_send[...] = jnp.sum(h_recv[...].astype(F32), axis=0).astype(BF16)

    arrive(w4_recv.at[pl.ds(0, nz - 1)], w4_s, w4_r)
    mine_at = w_fin.at[core, x * ny + y]
    mine_at[...] = jnp.sum(w4_recv[...].astype(F32), axis=0).astype(BF16)
    for i, j in plane:
        push(mine_at, mine_at, w5_s, w5_r, y_at(i) * CORES + core, z * nx + x_at(j))
    for k in far_z:
        push(h2_send.at[z_at(k)], h2_recv.at[z], gz_s, gz_r, me_d, z_at(k) * nx + x)
    h2_recv[z] = h2_send[z]

    arrive(g_ret.at[pl.ds(0, nd - 1)], gh_s, gh_r)
    own_grad = own_grad + mm(pick_t[...], g_ret[...].reshape(nd * slots, width))

    arrive(w_fin.at[core, pl.ds(0, len(plane))], w5_s, w5_r)
    push(w_fin.at[core], w_fin.at[core], w7_s, w7_r, sibling, me_g)

    arrive(h2_recv.at[pl.ds(0, nz - 1)], gz_s, gz_r)
    hub_total = jnp.sum(h2_recv[...].astype(F32), axis=0)
    hub_pick_t = jnp.where(
        lax.broadcasted_iota(jnp.int32, (nodes, hubs), 0).astype(F32) == jnp.broadcast_to(hub_index, (nodes, hubs)),
        1.0, 0.0).astype(BF16)
    high = hub_total.astype(BF16)
    low = (hub_total - high.astype(F32)).astype(BF16)
    grad_feat[...] = (own_grad + mm(hub_pick_t, high) + mm(hub_pick_t, low)).astype(BF16)
    stores.append(pltpu.make_async_copy(grad_feat, grad_feat_to, store_sem.at[1]))
    stores[-1].start()

    arrive(w_fin.at[core], w7_s, w7_r)
    stores.append(pltpu.make_async_copy(w_fin, w_fin_to, store_sem.at[2]))
    stores[-1].start()
    sent(hub_in.at[0, pl.ds(0, nz - 1)], hz_s, hz_r.at[0])
    sent(hub_in.at[pl.ds(0, nx - 1)], hx_s, hx_r)
    sent(out_send.at[pl.ds(0, nd - 1)], halo_s, halo_r)
    sent(gw, w1_s, w1_r)
    sent(h_send.at[pl.ds(0, nx - 1)], gx_s, gx_r)
    sent(w2_send.at[pl.ds(0, len(plane))], w2_s, w2_r)
    sent(w4_recv.at[pl.ds(0, nz - 1)], w4_s, w4_r)
    sent(g_send.at[pl.ds(0, nd - 1)], gh_s, gh_r)
    sent(w_fin.at[core, pl.ds(0, len(plane))], w5_s, w5_r)
    sent(h2_send.at[pl.ds(0, nz - 1)], gz_s, gz_r)
    sent(w_fin.at[core], w7_s, w7_r)
    for copy in stores:
        copy.wait()


def store(ny, out_in, grad_in, w_in, out_to, grad_to, self_to, neigh_to, out, grad, w_fin, grad_self, grad_neigh, load_sem, store_sem):
    loads = [
        pltpu.make_async_copy(src, via, load_sem.at[i])
        for i, (src, via) in enumerate(((w_in, w_fin), (out_in, out), (grad_in, grad)))]
    stores = [
        pltpu.make_async_copy(via, dst, store_sem.at[i])
        for i, (via, dst) in enumerate(((grad_self, self_to), (grad_neigh, neigh_to), (out, out_to), (grad, grad_to)))]
    for load in loads:
        load.start()
    for load in loads:
        load.wait()
    stores[2].start()
    stores[3].start()
    _, blocks, crows, _ = w_fin.shape
    nx = blocks // ny
    for matrix, result in enumerate((grad_self, grad_neigh)):
        for j in range(nx):
            for i in range(ny):
                top = (i * (nx // 2) + j // 2) * crows
                result[top:top + crows, (j % 2) * 128:(j % 2) * 128 + 128] = w_fin[matrix, j * ny + i].astype(F32)
        stores[matrix].start()
    for copy in stores:
        copy.wait()


def on_device(dims, features, w_self, w_neigh, adjacency, tile_ids, send_rows, send_counts, hub_rows, cotangent):
    nd, ny, nz, nx = dims
    nodes, width = features.shape
    row_tiles, _, tile, _ = adjacency.shape
    slots, hubs = send_rows.shape[1], hub_rows.shape[1]
    src_tiles = (nodes + nd * slots + nz * nx * hubs) // tile
    crows = nodes // ny // (nx // 2)
    args = (features, w_self, w_neigh, adjacency, tile_ids, send_rows, send_counts, hub_rows, cotangent)
    hbm = pl.BlockSpec(memory_space=pltpu.HBM)
    dma = pltpu.SemaphoreType.DMA
    results = pl.pallas_call(
        functools.partial(kernel, dims),
        out_shape=(
            jax.ShapeDtypeStruct((nodes, width), BF16),
            jax.ShapeDtypeStruct((nodes, width), BF16),
            jax.ShapeDtypeStruct((2, nx * ny, crows, 128), BF16),
        ),
        in_specs=[hbm] * len(args),
        out_specs=[hbm] * 3,
        scratch_shapes=[
            (pltpu.SMEM if arg is tile_ids else pltpu.VMEM)(arg.shape, arg.dtype) for arg in args
        ] + [
            dma((len(args),)),
            pltpu.VMEM((nodes, width), BF16),
            pltpu.VMEM((nodes, width), BF16),
            dma((3,)),
            pltpu.VMEM((nd, slots, width), BF16),
            pltpu.VMEM((nd, slots, width), BF16),
            pltpu.VMEM((hubs, width), BF16),
            pltpu.VMEM((nx, nz, hubs, width), BF16),
            pltpu.VMEM((src_tiles, nodes, tile), BF16),
            pltpu.VMEM((src_tiles, tile, nodes), BF16),
            pltpu.VMEM((src_tiles, nodes, tile), BF16),
            pltpu.VMEM((src_tiles, tile, nodes), BF16),
            pltpu.VMEM((nd * slots, nodes), BF16),
            pltpu.VMEM((nodes, nd * slots), BF16),
            pltpu.VMEM((2, width, nodes), BF16),
            pltpu.VMEM((nd, slots, width), BF16),
            pltpu.VMEM((nd, slots, width), BF16),
            pltpu.VMEM((nx, nz, hubs, width), BF16),
            pltpu.VMEM((nx, nz, hubs, width), BF16),
            pltpu.VMEM((nz, hubs, width), BF16),
            pltpu.VMEM((nz, hubs, width), BF16),
            pltpu.VMEM((width, width), F32),
            pltpu.VMEM((width, width), F32),
            pltpu.VMEM((ny * nx, crows, 128), BF16),
            pltpu.VMEM((ny * nx, crows, 128), BF16),
            pltpu.VMEM((nz, crows, 128), BF16),
            pltpu.VMEM((2, nx * ny, crows, 128), BF16),
        ] + [dma] * 3 + [dma((4,))] + [dma] * 18,
        compiler_params=pltpu.CompilerParams(
            collective_id=0, has_side_effects=True, vmem_limit_bytes=VMEM_LIMIT),
    )(*args)
    rows = jax.ShapeDtypeStruct((nodes, width), BF16)
    weights = jax.ShapeDtypeStruct((width, width), F32)
    return pl.pallas_call(
        functools.partial(store, ny),
        out_shape=(rows, rows, weights, weights),
        in_specs=[hbm] * 3,
        out_specs=[hbm] * 4,
        scratch_shapes=[pltpu.VMEM(r.shape, r.dtype) for r in (*results, weights, weights)] + [dma((3,)), dma((4,))],
        compiler_params=pltpu.CompilerParams(vmem_limit_bytes=VMEM_LIMIT),
    )(*results)


def solution(mesh):
    nd, ng = mesh.shape["dom"], mesh.shape["grp"]
    dims = (nd, nd // CORES, ng // X_CHIPS, X_CHIPS)
    placed = (
        P(("dom", "grp"), None),
        P(),
        P(),
        P(("dom", "grp"), None, None, None),
        P(("dom", "grp"), None),
        P(("dom", "grp"), None),
        P(("dom", "grp"), None),
        P(("dom", "grp"), None),
        P(("dom", "grp"), None),
    )
    return jax.shard_map(
        functools.partial(on_device, dims),
        mesh=mesh,
        in_specs=placed,
        out_specs=(P(("dom", "grp"), None), P(("dom", "grp"), None), P(), P()),
        check_vma=False,
    )
```

```python
import functools

import jax
import jax.numpy as jnp
from jax import lax
from jax.experimental import pallas as pl
from jax.experimental.pallas import tpu as pltpu
from jax.sharding import PartitionSpec as P

CORES = 2
X_CHIPS = 4

VMEM_LIMIT = 60 * 1024 * 1024

F32 = jnp.float32
BF16 = jnp.bfloat16


def mm(a, b):
    return jnp.dot(a, b, preferred_element_type=F32)


def mm_nt(a, b):
    return lax.dot_general(a, b, (((1,), (1,)), ((), ())), preferred_element_type=F32)


def far_first(*sizes):
    offsets = [()]
    for size in sizes:
        offsets = [o + (k,) for o in offsets for k in range(size)]
    hops = lambda o: sum(min(k, size - k) for k, size in zip(o, sizes))
    return sorted((o for o in offsets if any(o)), key=lambda o: -hops(o))


def kernel(
    dims,
    feat_in, w_self_in, w_neigh_in, adj_in, ids_in, send_rows_in, send_counts_in, hub_rows_in, cot_in,
    out_to, grad_feat_to, w_fin_to,
    feat, w_self, w_neigh, adj, ids, send_rows, send_counts, hub_rows, cot, load_sem,
    out, grad_feat, store_sem,
    out_send, halo_in, hub_own, hub_in, dense, dense_t, dense_low, dense_low_t, pick, pick_t, lhs_t,
    g_send, g_ret, h_send, h_recv, h2_send, h2_recv,
    gw, w_sib, w2_send, w2_recv, w4_recv, w_fin,
    halo_s, halo_r, hz_s, hz_r, hx_s, hx_r, gh_s, gh_r, gx_s, gx_r, gz_s, gz_r,
    w1_s, w1_r, w2_s, w2_r, w4_s, w4_r, w5_s, w5_r, w7_s, w7_r,
):
    nd, ny, nz, nx = dims
    nodes, width = feat.shape
    row_tiles, per_row, tile, _ = adj.shape
    slots = send_rows.shape[1]
    hubs = hub_rows.shape[1]
    src_tiles = dense.shape[0]
    own_tiles = nodes // tile
    halo_tiles = nd * slots // tile
    crows = w_fin.shape[2]
    me_d = lax.axis_index("dom")
    me_g = lax.axis_index("grp")
    y, core = lax.div(me_d, CORES), lax.rem(me_d, CORES)
    z, x = lax.div(me_g, nx), lax.rem(me_g, nx)

    def dom_at(k):
        return lax.rem(me_d + k, nd)

    def z_at(k):
        return lax.rem(z + k, nz)

    def x_at(k):
        return lax.rem(x + k, nx)

    def y_at(k):
        return lax.rem(y + k, ny)

    sibling = y * CORES + (1 - core)
    def copy_of(src, dst, send_sem, recv_sem, d, g):
        return pltpu.make_async_remote_copy(
            src_ref=src, dst_ref=dst, send_sem=send_sem, recv_sem=recv_sem,
            device_id=(d, g), device_id_type=pl.DeviceIdType.MESH,
        )

    def push(*copy):
        copy_of(*copy).start()

    def arrive(size, send_sem, recv_sem):
        copy_of(size, size, send_sem, recv_sem, sibling, me_g).wait_recv()

    def sent(size, send_sem, recv_sem):
        copy_of(size, size, send_sem, recv_sem, sibling, me_g).wait_send()

    loads = [
        pltpu.make_async_copy(src, dst, load_sem.at[i])
        for i, (src, dst) in enumerate((
            (hub_rows_in, hub_rows), (feat_in, feat), (send_counts_in, send_counts), (send_rows_in, send_rows),
            (ids_in, ids), (adj_in, adj), (w_self_in, w_self), (w_neigh_in, w_neigh), (cot_in, cot)))
    ]
    for load in loads:
        load.start()

    barrier = pltpu.get_barrier_semaphore()
    far_z = [k for (k,) in far_first(nz)]
    far_x = [k for (k,) in far_first(nx)]
    far_dom = [i * CORES + j for i, j in far_first(ny, CORES)]
    partners = [(me_d, z_at(k) * nx + x) for k in far_z]
    partners += [(me_d, z * nx + x_at(k)) for k in far_x]
    partners += [(dom_at(k), me_g) for k in far_dom]
    for partner in partners:
        pl.semaphore_signal(barrier, inc=1, device_id=partner, device_id_type=pl.DeviceIdType.MESH)

    z_group = nz // 3
    for load in loads[:2]:
        load.wait()
    features = feat[...]
    hub_index = hub_rows[...].astype(F32)
    hub_eye = lax.broadcasted_iota(jnp.int32, (hubs, hubs), 0) == lax.broadcasted_iota(jnp.int32, (hubs, hubs), 1)
    hub_col = jnp.sum(
        jnp.where(hub_eye, jnp.broadcast_to(hub_index, (hubs, hubs)), 0.0), axis=1, keepdims=True)
    hub_pick = jnp.where(
        lax.broadcasted_iota(jnp.int32, (hubs, nodes), 1).astype(F32) == hub_col, 1.0, 0.0).astype(BF16)
    hub_own[...] = mm(hub_pick, features).astype(BF16)

    for load in loads[2:4]:
        load.wait()
    count_col = jnp.sum(
        jnp.where(
            lax.broadcasted_iota(jnp.int32, (nd, nd), 0) == lax.broadcasted_iota(jnp.int32, (nd, nd), 1),
            jnp.broadcast_to(send_counts[...], (nd, nd)), 0).astype(F32),
        axis=1, keepdims=True)
    live = lax.broadcasted_iota(jnp.int32, (nd, slots), 1).astype(F32) < count_col
    index = jnp.where(live, send_rows[...].astype(F32), -1.0)
    total_slots = nd * slots
    slot = lax.broadcasted_iota(jnp.int32, (total_slots, slots), 0)
    own_part = lax.div(lax.broadcasted_iota(jnp.int32, (total_slots, nd), 0), slots) == lax.broadcasted_iota(
        jnp.int32, (total_slots, nd), 1)
    spread = mm(jnp.where(own_part, 1.0, 0.0).astype(BF16), index.astype(BF16))
    spread = jnp.where(lax.rem(slot, slots) == lax.broadcasted_iota(jnp.int32, (total_slots, slots), 1), spread, 0.0)
    spread = mm(spread.astype(BF16), jnp.ones((slots, nodes), BF16))
    lane = lax.broadcasted_iota(jnp.int32, (total_slots, nodes), 1).astype(F32)
    pick[...] = jnp.where(lane == spread, 1.0, 0.0).astype(BF16)
    out_send[...] = mm(pick[...], features).astype(BF16).reshape(nd, slots, width)
    halo_in[me_d] = out_send[me_d]
    pl.semaphore_wait(barrier, len(partners))

    for k in far_z:
        push(hub_own, hub_in.at[x, z], hz_s, hz_r.at[lax.div(z, z_group)], me_d, z_at(k) * nx + x)
    pltpu.make_async_copy(hub_own, hub_in.at[x, z], hz_r.at[lax.div(z, z_group)]).start()
    for k in far_dom:
        push(out_send.at[dom_at(k)], halo_in.at[me_d], halo_s, halo_r, dom_at(k), me_g)

    def gather_tiles(c, carry):
        parts = []
        for r in range(row_tiles):
            total = jnp.zeros((tile, tile), F32)
            for t in range(per_row):
                total = total + jnp.where(ids[r, t] == c, adj[r, t].astype(F32), 0.0)
            parts.append(total)
        block = jnp.concatenate(parts, axis=0)
        high = block.astype(BF16)
        low = block - high.astype(F32)
        dense[c] = high
        dense_low[c] = low.astype(BF16)
        dense_t[c] = high.astype(F32).T.astype(BF16)
        dense_low_t[c] = low.T.astype(BF16)
        return carry

    for load in loads[4:]:
        load.wait()
    lax.fori_loop(0, src_tiles, gather_tiles, 0)

    for group in range(3):
        block = hub_in.at[x, pl.ds(group * z_group, z_group)]
        arrive(block, hz_s, hz_r.at[group])
        for j in far_x:
            push(block, block, hx_s, hx_r, me_d, z * nx + x_at(j))

    sums = []
    for r in range(row_tiles):
        total = jnp.zeros((tile, tile), F32)
        for t in range(per_row):
            total = total + adj[r, t].astype(F32)
        sums.append(jnp.sum(total, axis=1, keepdims=True))
    inverse = 1.0 / (1.0 + jnp.concatenate(sums, axis=0))
    lhs_t[0] = features.astype(F32).T.astype(BF16)
    pick_t[...] = pick[...].astype(F32).T.astype(BF16)

    def from_tiles(first, count, rows):
        return sum(
            mm(jnp.concatenate([part[c] for c in range(first, first + count)], axis=1), rows)
            for part in (dense, dense_low))

    def to_tiles(first, count, rows):
        return sum(
            mm(part[first:first + count].reshape(count * tile, nodes), rows) for part in (dense_t, dense_low_t))

    numer = from_tiles(0, own_tiles, features)
    pre = mm(features, w_self[...])
    arrive(halo_in.at[pl.ds(0, nd - 1)], halo_s, halo_r)
    numer = numer + from_tiles(own_tiles, halo_tiles, halo_in[...].reshape(nd * slots, width))
    arrive(hub_in.at[pl.ds(0, nx - 1)], hx_s, hx_r)
    hub_rows_all = jnp.concatenate(
        [hub_in[j, i] for i in range(nz) for j in range(nx)], axis=0)
    hub_tiles = src_tiles - own_tiles - halo_tiles
    numer = numer + from_tiles(own_tiles + halo_tiles, hub_tiles, hub_rows_all)
    agg = numer * inverse
    agg_b = agg.astype(BF16)
    pre = pre + mm(agg_b, w_neigh[...])
    sig = 1.0 / (1.0 + jnp.exp(-pre))
    out[...] = (pre * sig).astype(BF16)
    stores = [pltpu.make_async_copy(out, out_to, store_sem.at[0])]
    stores[-1].start()
    grad_pre = (cot[...].astype(F32) * sig * (1.0 + pre * (1.0 - sig))).astype(BF16)

    lhs_t[1] = agg_b.astype(F32).T.astype(BF16)
    gw[...] = mm(lhs_t[1 - core], grad_pre)
    push(gw, w_sib, w1_s, w1_r, sibling, me_g)
    mine = mm(lhs_t[core], grad_pre)

    grad_num = (mm_nt(grad_pre, w_neigh[...]) * inverse).astype(BF16)
    hub_grad = to_tiles(own_tiles + halo_tiles, hub_tiles, grad_num).astype(BF16)
    for g in range(nz * nx):
        h_send[g % nx, g // nx] = hub_grad[g * hubs:(g + 1) * hubs, :]
    for j in far_x:
        push(h_send.at[x_at(j)], h_recv.at[x], gx_s, gx_r, me_d, z * nx + x_at(j))
    h_recv[x] = h_send[x]
    g_send[...] = to_tiles(own_tiles, halo_tiles, grad_num).astype(BF16).reshape(nd, slots, width)

    arrive(w_sib, w1_s, w1_r)
    mine = mine + w_sib[...]
    yrows = nodes // ny
    plane = far_first(ny, nx)
    for i in range(ny):
        for j in range(nx):
            top = i * yrows + (j // 2) * crows
            w2_send[i * nx + j] = mine[top:top + crows, (j % 2) * 128:(j % 2) * 128 + 128].astype(BF16)
    for n, (i, j) in enumerate(plane):
        push(w2_send.at[y_at(i) * nx + x_at(j)], w2_recv.at[n + 1], w2_s, w2_r, y_at(i) * CORES + core,
             z * nx + x_at(j))
    w2_recv[0] = w2_send[y * nx + x]
    own_grad = mm_nt(grad_pre, w_self[...]) + to_tiles(0, own_tiles, grad_num)

    arrive(w2_recv.at[pl.ds(1, len(plane))], w2_s, w2_r)
    w4_recv[z] = jnp.sum(w2_recv[...].astype(F32), axis=0).astype(BF16)
    for k in far_z:
        push(w4_recv.at[z], w4_recv.at[z], w4_s, w4_r, me_d, z_at(k) * nx + x)
    for k in far_dom:
        push(g_send.at[dom_at(k)], g_ret.at[me_d], gh_s, gh_r, dom_at(k), me_g)
    g_ret[me_d] = g_send[me_d]

    arrive(h_recv.at[pl.ds(0, nx - 1)], gx_s, gx_r)
    h2_send[...] = jnp.sum(h_recv[...].astype(F32), axis=0).astype(BF16)

    arrive(w4_recv.at[pl.ds(0, nz - 1)], w4_s, w4_r)
    mine_at = w_fin.at[core, x * ny + y]
    mine_at[...] = jnp.sum(w4_recv[...].astype(F32), axis=0).astype(BF16)
    for i, j in plane:
        push(mine_at, mine_at, w5_s, w5_r, y_at(i) * CORES + core, z * nx + x_at(j))
    for k in far_z:
        push(h2_send.at[z_at(k)], h2_recv.at[z], gz_s, gz_r, me_d, z_at(k) * nx + x)
    h2_recv[z] = h2_send[z]

    arrive(g_ret.at[pl.ds(0, nd - 1)], gh_s, gh_r)
    own_grad = own_grad + mm(pick_t[...], g_ret[...].reshape(nd * slots, width))

    arrive(w_fin.at[core, pl.ds(0, len(plane))], w5_s, w5_r)
    push(w_fin.at[core], w_fin.at[core], w7_s, w7_r, sibling, me_g)

    arrive(h2_recv.at[pl.ds(0, nz - 1)], gz_s, gz_r)
    hub_total = jnp.sum(h2_recv[...].astype(F32), axis=0)
    hub_pick_t = jnp.where(
        lax.broadcasted_iota(jnp.int32, (nodes, hubs), 0).astype(F32) == jnp.broadcast_to(hub_index, (nodes, hubs)),
        1.0, 0.0).astype(BF16)
    high = hub_total.astype(BF16)
    low = (hub_total - high.astype(F32)).astype(BF16)
    grad_feat[...] = (own_grad + mm(hub_pick_t, high) + mm(hub_pick_t, low)).astype(BF16)
    stores.append(pltpu.make_async_copy(grad_feat, grad_feat_to, store_sem.at[1]))
    stores[-1].start()

    arrive(w_fin.at[core], w7_s, w7_r)
    stores.append(pltpu.make_async_copy(w_fin, w_fin_to, store_sem.at[2]))
    stores[-1].start()
    sent(hub_in.at[0, pl.ds(0, nz - 1)], hz_s, hz_r.at[0])
    sent(hub_in.at[pl.ds(0, nx - 1)], hx_s, hx_r)
    sent(out_send.at[pl.ds(0, nd - 1)], halo_s, halo_r)
    sent(gw, w1_s, w1_r)
    sent(h_send.at[pl.ds(0, nx - 1)], gx_s, gx_r)
    sent(w2_send.at[pl.ds(0, len(plane))], w2_s, w2_r)
    sent(w4_recv.at[pl.ds(0, nz - 1)], w4_s, w4_r)
    sent(g_send.at[pl.ds(0, nd - 1)], gh_s, gh_r)
    sent(w_fin.at[core, pl.ds(0, len(plane))], w5_s, w5_r)
    sent(h2_send.at[pl.ds(0, nz - 1)], gz_s, gz_r)
    sent(w_fin.at[core], w7_s, w7_r)
    for copy in stores:
        copy.wait()


def store(ny, out_in, grad_in, w_in, out_to, grad_to, self_to, neigh_to, out, grad, w_fin, grad_self, grad_neigh, load_sem, store_sem):
    loads = [
        pltpu.make_async_copy(src, via, load_sem.at[i])
        for i, (src, via) in enumerate(((w_in, w_fin), (out_in, out), (grad_in, grad)))]
    stores = [
        pltpu.make_async_copy(via, dst, store_sem.at[i])
        for i, (via, dst) in enumerate(((grad_self, self_to), (grad_neigh, neigh_to), (out, out_to), (grad, grad_to)))]
    for load in loads:
        load.start()
    loads[0].wait()
    _, blocks, crows, _ = w_fin.shape
    nx = blocks // ny
    for matrix, result in enumerate((grad_self, grad_neigh)):
        for j in range(nx):
            for i in range(ny):
                top = (i * (nx // 2) + j // 2) * crows
                result[top:top + crows, (j % 2) * 128:(j % 2) * 128 + 128] = w_fin[matrix, j * ny + i].astype(F32)
        stores[matrix].start()
        loads[matrix + 1].wait()
        stores[matrix + 2].start()
    for copy in stores:
        copy.wait()


def on_device(dims, features, w_self, w_neigh, adjacency, tile_ids, send_rows, send_counts, hub_rows, cotangent):
    nd, ny, nz, nx = dims
    nodes, width = features.shape
    row_tiles, _, tile, _ = adjacency.shape
    slots, hubs = send_rows.shape[1], hub_rows.shape[1]
    src_tiles = (nodes + nd * slots + nz * nx * hubs) // tile
    crows = nodes // ny // (nx // 2)
    args = (features, w_self, w_neigh, adjacency, tile_ids, send_rows, send_counts, hub_rows, cotangent)
    hbm = pl.BlockSpec(memory_space=pltpu.HBM)
    dma = pltpu.SemaphoreType.DMA
    results = pl.pallas_call(
        functools.partial(kernel, dims),
        out_shape=(
            jax.ShapeDtypeStruct((nodes, width), BF16),
            jax.ShapeDtypeStruct((nodes, width), BF16),
            jax.ShapeDtypeStruct((2, nx * ny, crows, 128), BF16),
        ),
        in_specs=[hbm] * len(args),
        out_specs=[hbm] * 3,
        scratch_shapes=[
            (pltpu.SMEM if arg is tile_ids else pltpu.VMEM)(arg.shape, arg.dtype) for arg in args
        ] + [
            dma((len(args),)),
            pltpu.VMEM((nodes, width), BF16),
            pltpu.VMEM((nodes, width), BF16),
            dma((3,)),
            pltpu.VMEM((nd, slots, width), BF16),
            pltpu.VMEM((nd, slots, width), BF16),
            pltpu.VMEM((hubs, width), BF16),
            pltpu.VMEM((nx, nz, hubs, width), BF16),
            pltpu.VMEM((src_tiles, nodes, tile), BF16),
            pltpu.VMEM((src_tiles, tile, nodes), BF16),
            pltpu.VMEM((src_tiles, nodes, tile), BF16),
            pltpu.VMEM((src_tiles, tile, nodes), BF16),
            pltpu.VMEM((nd * slots, nodes), BF16),
            pltpu.VMEM((nodes, nd * slots), BF16),
            pltpu.VMEM((2, width, nodes), BF16),
            pltpu.VMEM((nd, slots, width), BF16),
            pltpu.VMEM((nd, slots, width), BF16),
            pltpu.VMEM((nx, nz, hubs, width), BF16),
            pltpu.VMEM((nx, nz, hubs, width), BF16),
            pltpu.VMEM((nz, hubs, width), BF16),
            pltpu.VMEM((nz, hubs, width), BF16),
            pltpu.VMEM((width, width), F32),
            pltpu.VMEM((width, width), F32),
            pltpu.VMEM((ny * nx, crows, 128), BF16),
            pltpu.VMEM((ny * nx, crows, 128), BF16),
            pltpu.VMEM((nz, crows, 128), BF16),
            pltpu.VMEM((2, nx * ny, crows, 128), BF16),
        ] + [dma] * 3 + [dma((3,))] + [dma] * 18,
        compiler_params=pltpu.CompilerParams(
            collective_id=0, has_side_effects=True, vmem_limit_bytes=VMEM_LIMIT),
    )(*args)
    rows = jax.ShapeDtypeStruct((nodes, width), BF16)
    weights = jax.ShapeDtypeStruct((width, width), F32)
    return pl.pallas_call(
        functools.partial(store, ny),
        out_shape=(rows, rows, weights, weights),
        in_specs=[hbm] * 3,
        out_specs=[hbm] * 4,
        scratch_shapes=[pltpu.VMEM(r.shape, r.dtype) for r in (*results, weights, weights)] + [dma((3,)), dma((4,))],
        compiler_params=pltpu.CompilerParams(vmem_limit_bytes=VMEM_LIMIT),
    )(*results)


def solution(mesh):
    nd, ng = mesh.shape["dom"], mesh.shape["grp"]
    dims = (nd, nd // CORES, ng // X_CHIPS, X_CHIPS)
    placed = (
        P(("dom", "grp"), None),
        P(),
        P(),
        P(("dom", "grp"), None, None, None),
        P(("dom", "grp"), None),
        P(("dom", "grp"), None),
        P(("dom", "grp"), None),
        P(("dom", "grp"), None),
        P(("dom", "grp"), None),
    )
    return jax.shard_map(
        functools.partial(on_device, dims),
        mesh=mesh,
        in_specs=placed,
        out_specs=(P(("dom", "grp"), None), P(("dom", "grp"), None), P(), P()),
        check_vma=False,
    )
```

```python
import functools

import jax
import jax.numpy as jnp
from jax import lax
from jax.experimental import pallas as pl
from jax.experimental.pallas import tpu as pltpu
from jax.sharding import PartitionSpec as P

CORES = 2
X_CHIPS = 4

VMEM_LIMIT = 60 * 1024 * 1024

F32 = jnp.float32
BF16 = jnp.bfloat16


def mm(a, b):
    return jnp.dot(a, b, preferred_element_type=F32)


def mm_nt(a, b):
    return lax.dot_general(a, b, (((1,), (1,)), ((), ())), preferred_element_type=F32)


def far_first(*sizes):
    offsets = [()]
    for size in sizes:
        offsets = [o + (k,) for o in offsets for k in range(size)]
    hops = lambda o: sum(min(k, size - k) for k, size in zip(o, sizes))
    return sorted((o for o in offsets if any(o)), key=lambda o: -hops(o))


def kernel(
    dims,
    feat_in, w_self_in, w_neigh_in, adj_in, ids_in, send_rows_in, send_counts_in, hub_rows_in, cot_in,
    out_to, grad_feat_to, w_fin_to,
    feat, w_self, w_neigh, adj, ids, send_rows, send_counts, hub_rows, cot, load_sem,
    out, grad_feat, store_sem,
    out_send, halo_in, hub_own, hub_in, dense, dense_t, dense_low, dense_low_t, pick, pick_t, lhs_t,
    g_send, g_ret, h_send, h_recv, h2_send, h2_recv,
    gw, w_sib, w2_send, w2_recv, w4_recv, w_fin,
    halo_s, halo_r, hz_s, hz_r, hx_s, hx_r, gh_s, gh_r, gx_s, gx_r, gz_s, gz_r,
    w1_s, w1_r, w2_s, w2_r, w4_s, w4_r, w5_s, w5_r, w7_s, w7_r,
):
    nd, ny, nz, nx = dims
    nodes, width = feat.shape
    row_tiles, per_row, tile, _ = adj.shape
    slots = send_rows.shape[1]
    hubs = hub_rows.shape[1]
    src_tiles = dense.shape[0]
    own_tiles = nodes // tile
    halo_tiles = nd * slots // tile
    crows = w_fin.shape[2]
    me_d = lax.axis_index("dom")
    me_g = lax.axis_index("grp")
    y, core = lax.div(me_d, CORES), lax.rem(me_d, CORES)
    z, x = lax.div(me_g, nx), lax.rem(me_g, nx)

    def dom_at(k):
        return lax.rem(me_d + k, nd)

    def z_at(k):
        return lax.rem(z + k, nz)

    def x_at(k):
        return lax.rem(x + k, nx)

    def y_at(k):
        return lax.rem(y + k, ny)

    sibling = y * CORES + (1 - core)
    def copy_of(src, dst, send_sem, recv_sem, d, g):
        return pltpu.make_async_remote_copy(
            src_ref=src, dst_ref=dst, send_sem=send_sem, recv_sem=recv_sem,
            device_id=(d, g), device_id_type=pl.DeviceIdType.MESH,
        )

    def push(*copy):
        copy_of(*copy).start()

    def arrive(size, send_sem, recv_sem):
        copy_of(size, size, send_sem, recv_sem, sibling, me_g).wait_recv()

    def sent(size, send_sem, recv_sem):
        copy_of(size, size, send_sem, recv_sem, sibling, me_g).wait_send()

    loads = [
        pltpu.make_async_copy(src, dst, load_sem.at[i])
        for i, (src, dst) in enumerate((
            (hub_rows_in, hub_rows), (feat_in, feat), (send_counts_in, send_counts), (send_rows_in, send_rows),
            (ids_in, ids), (adj_in, adj), (w_self_in, w_self), (w_neigh_in, w_neigh), (cot_in, cot)))
    ]
    for load in loads:
        load.start()

    barrier = pltpu.get_barrier_semaphore()
    far_z = [k for (k,) in far_first(nz)]
    far_x = [k for (k,) in far_first(nx)]
    far_dom = [i * CORES + j for i, j in far_first(ny, CORES)]
    partners = [(me_d, z_at(k) * nx + x) for k in far_z]
    partners += [(me_d, z * nx + x_at(k)) for k in far_x]
    partners += [(dom_at(k), me_g) for k in far_dom]
    for partner in partners:
        pl.semaphore_signal(barrier, inc=1, device_id=partner, device_id_type=pl.DeviceIdType.MESH)

    z_group = nz // 3
    for load in loads[:2]:
        load.wait()
    features = feat[...]
    hub_index = hub_rows[...].astype(F32)
    hub_eye = lax.broadcasted_iota(jnp.int32, (hubs, hubs), 0) == lax.broadcasted_iota(jnp.int32, (hubs, hubs), 1)
    hub_col = jnp.sum(
        jnp.where(hub_eye, jnp.broadcast_to(hub_index, (hubs, hubs)), 0.0), axis=1, keepdims=True)
    hub_pick = jnp.where(
        lax.broadcasted_iota(jnp.int32, (hubs, nodes), 1).astype(F32) == hub_col, 1.0, 0.0).astype(BF16)
    hub_own[...] = mm(hub_pick, features).astype(BF16)

    for load in loads[2:4]:
        load.wait()
    count_col = jnp.sum(
        jnp.where(
            lax.broadcasted_iota(jnp.int32, (nd, nd), 0) == lax.broadcasted_iota(jnp.int32, (nd, nd), 1),
            jnp.broadcast_to(send_counts[...], (nd, nd)), 0).astype(F32),
        axis=1, keepdims=True)
    live = lax.broadcasted_iota(jnp.int32, (nd, slots), 1).astype(F32) < count_col
    index = jnp.where(live, send_rows[...].astype(F32), -1.0)
    total_slots = nd * slots
    slot = lax.broadcasted_iota(jnp.int32, (total_slots, slots), 0)
    own_part = lax.div(lax.broadcasted_iota(jnp.int32, (total_slots, nd), 0), slots) == lax.broadcasted_iota(
        jnp.int32, (total_slots, nd), 1)
    spread = mm(jnp.where(own_part, 1.0, 0.0).astype(BF16), index.astype(BF16))
    spread = jnp.where(lax.rem(slot, slots) == lax.broadcasted_iota(jnp.int32, (total_slots, slots), 1), spread, 0.0)
    spread = mm(spread.astype(BF16), jnp.ones((slots, nodes), BF16))
    lane = lax.broadcasted_iota(jnp.int32, (total_slots, nodes), 1).astype(F32)
    pick[...] = jnp.where(lane == spread, 1.0, 0.0).astype(BF16)
    out_send[...] = mm(pick[...], features).astype(BF16).reshape(nd, slots, width)
    halo_in[me_d] = out_send[me_d]
    pl.semaphore_wait(barrier, len(partners))

    for k in far_z:
        push(hub_own, hub_in.at[x, z], hz_s, hz_r.at[lax.div(z, z_group)], me_d, z_at(k) * nx + x)
    pltpu.make_async_copy(hub_own, hub_in.at[x, z], hz_r.at[lax.div(z, z_group)]).start()
    for k in far_dom:
        push(out_send.at[dom_at(k)], halo_in.at[me_d], halo_s, halo_r, dom_at(k), me_g)

    def gather_tiles(c, carry):
        parts = []
        for r in range(row_tiles):
            total = jnp.zeros((tile, tile), F32)
            for t in range(per_row):
                total = total + jnp.where(ids[r, t] == c, adj[r, t].astype(F32), 0.0)
            parts.append(total)
        block = jnp.concatenate(parts, axis=0)
        high = block.astype(BF16)
        low = block - high.astype(F32)
        dense[c] = high
        dense_low[c] = low.astype(BF16)
        dense_t[c] = high.astype(F32).T.astype(BF16)
        dense_low_t[c] = low.T.astype(BF16)
        return carry

    for load in loads[4:]:
        load.wait()
    lax.fori_loop(0, src_tiles, gather_tiles, 0)

    for group in range(3):
        block = hub_in.at[x, pl.ds(group * z_group, z_group)]
        arrive(block, hz_s, hz_r.at[group])
        for j in far_x:
            push(block, block, hx_s, hx_r, me_d, z * nx + x_at(j))

    sums = []
    for r in range(row_tiles):
        total = jnp.zeros((tile, tile), F32)
        for t in range(per_row):
            total = total + adj[r, t].astype(F32)
        sums.append(jnp.sum(total, axis=1, keepdims=True))
    inverse = 1.0 / (1.0 + jnp.concatenate(sums, axis=0))
    lhs_t[0] = features.astype(F32).T.astype(BF16)
    pick_t[...] = pick[...].astype(F32).T.astype(BF16)

    def from_tiles(first, count, rows):
        return sum(
            mm(jnp.concatenate([part[c] for c in range(first, first + count)], axis=1), rows)
            for part in (dense, dense_low))

    def to_tiles(first, count, rows):
        return sum(
            mm(part[first:first + count].reshape(count * tile, nodes), rows) for part in (dense_t, dense_low_t))

    numer = from_tiles(0, own_tiles, features)
    pre = mm(features, w_self[...])
    arrive(halo_in.at[pl.ds(0, nd - 1)], halo_s, halo_r)
    numer = numer + from_tiles(own_tiles, halo_tiles, halo_in[...].reshape(nd * slots, width))
    arrive(hub_in.at[pl.ds(0, nx - 1)], hx_s, hx_r)
    hub_rows_all = jnp.concatenate(
        [hub_in[j, i] for i in range(nz) for j in range(nx)], axis=0)
    hub_tiles = src_tiles - own_tiles - halo_tiles
    numer = numer + from_tiles(own_tiles + halo_tiles, hub_tiles, hub_rows_all)
    agg = numer * inverse
    agg_b = agg.astype(BF16)
    pre = pre + mm(agg_b, w_neigh[...])
    sig = 1.0 / (1.0 + jnp.exp(-pre))
    out[...] = (pre * sig).astype(BF16)
    stores = [pltpu.make_async_copy(out, out_to, store_sem.at[0])]
    stores[-1].start()
    grad_pre = (cot[...].astype(F32) * sig * (1.0 + pre * (1.0 - sig))).astype(BF16)

    lhs_t[1] = agg_b.astype(F32).T.astype(BF16)
    gw[...] = mm(lhs_t[1 - core], grad_pre)
    push(gw, w_sib, w1_s, w1_r, sibling, me_g)
    mine = mm(lhs_t[core], grad_pre)

    grad_num = (mm_nt(grad_pre, w_neigh[...]) * inverse).astype(BF16)
    hub_grad = to_tiles(own_tiles + halo_tiles, hub_tiles, grad_num).astype(BF16)
    for g in range(nz * nx):
        h_send[g % nx, g // nx] = hub_grad[g * hubs:(g + 1) * hubs, :]
    for j in far_x:
        push(h_send.at[x_at(j)], h_recv.at[x], gx_s, gx_r, me_d, z * nx + x_at(j))
    h_recv[x] = h_send[x]
    g_send[...] = to_tiles(own_tiles, halo_tiles, grad_num).astype(BF16).reshape(nd, slots, width)

    arrive(w_sib, w1_s, w1_r)
    mine = mine + w_sib[...]
    yrows = nodes // ny
    plane = far_first(ny, nx)
    for i in range(ny):
        for j in range(nx):
            top = i * yrows + (j // 2) * crows
            w2_send[i * nx + j] = mine[top:top + crows, (j % 2) * 128:(j % 2) * 128 + 128].astype(BF16)
    for n, (i, j) in enumerate(plane):
        push(w2_send.at[y_at(i) * nx + x_at(j)], w2_recv.at[n + 1], w2_s, w2_r, y_at(i) * CORES + core,
             z * nx + x_at(j))
    w2_recv[0] = w2_send[y * nx + x]
    own_grad = mm_nt(grad_pre, w_self[...]) + to_tiles(0, own_tiles, grad_num)

    arrive(w2_recv.at[pl.ds(1, len(plane))], w2_s, w2_r)
    w4_recv[z] = jnp.sum(w2_recv[...].astype(F32), axis=0).astype(BF16)
    for k in far_z:
        push(w4_recv.at[z], w4_recv.at[z], w4_s, w4_r, me_d, z_at(k) * nx + x)
    for k in far_dom:
        push(g_send.at[dom_at(k)], g_ret.at[me_d], gh_s, gh_r, dom_at(k), me_g)
    g_ret[me_d] = g_send[me_d]

    arrive(h_recv.at[pl.ds(0, nx - 1)], gx_s, gx_r)
    h2_send[...] = jnp.sum(h_recv[...].astype(F32), axis=0).astype(BF16)

    arrive(w4_recv.at[pl.ds(0, nz - 1)], w4_s, w4_r)
    mine_at = w_fin.at[core, x * ny + y]
    mine_at[...] = jnp.sum(w4_recv[...].astype(F32), axis=0).astype(BF16)
    for i, j in plane:
        push(mine_at, mine_at, w5_s, w5_r, y_at(i) * CORES + core, z * nx + x_at(j))
    for k in far_z:
        push(h2_send.at[z_at(k)], h2_recv.at[z], gz_s, gz_r, me_d, z_at(k) * nx + x)
    h2_recv[z] = h2_send[z]

    arrive(g_ret.at[pl.ds(0, nd - 1)], gh_s, gh_r)
    own_grad = own_grad + mm(pick_t[...], g_ret[...].reshape(nd * slots, width))

    arrive(w_fin.at[core, pl.ds(0, len(plane))], w5_s, w5_r)
    push(w_fin.at[core], w_fin.at[core], w7_s, w7_r, sibling, me_g)
    stores.append(pltpu.make_async_copy(w_fin.at[core], w_fin_to.at[core], store_sem.at[3]))
    stores[-1].start()

    arrive(h2_recv.at[pl.ds(0, nz - 1)], gz_s, gz_r)
    hub_total = jnp.sum(h2_recv[...].astype(F32), axis=0)
    hub_pick_t = jnp.where(
        lax.broadcasted_iota(jnp.int32, (nodes, hubs), 0).astype(F32) == jnp.broadcast_to(hub_index, (nodes, hubs)),
        1.0, 0.0).astype(BF16)
    high = hub_total.astype(BF16)
    low = (hub_total - high.astype(F32)).astype(BF16)
    grad_feat[...] = (own_grad + mm(hub_pick_t, high) + mm(hub_pick_t, low)).astype(BF16)
    stores.append(pltpu.make_async_copy(grad_feat, grad_feat_to, store_sem.at[1]))
    stores[-1].start()

    arrive(w_fin.at[core], w7_s, w7_r)
    stores.append(pltpu.make_async_copy(w_fin.at[1 - core], w_fin_to.at[1 - core], store_sem.at[2]))
    stores[-1].start()
    sent(hub_in.at[0, pl.ds(0, nz - 1)], hz_s, hz_r.at[0])
    sent(hub_in.at[pl.ds(0, nx - 1)], hx_s, hx_r)
    sent(out_send.at[pl.ds(0, nd - 1)], halo_s, halo_r)
    sent(gw, w1_s, w1_r)
    sent(h_send.at[pl.ds(0, nx - 1)], gx_s, gx_r)
    sent(w2_send.at[pl.ds(0, len(plane))], w2_s, w2_r)
    sent(w4_recv.at[pl.ds(0, nz - 1)], w4_s, w4_r)
    sent(g_send.at[pl.ds(0, nd - 1)], gh_s, gh_r)
    sent(w_fin.at[core, pl.ds(0, len(plane))], w5_s, w5_r)
    sent(h2_send.at[pl.ds(0, nz - 1)], gz_s, gz_r)
    sent(w_fin.at[core], w7_s, w7_r)
    for copy in stores:
        copy.wait()


def store(ny, out_in, grad_in, w_in, out_to, grad_to, self_to, neigh_to, out, grad, w_fin, grad_self, grad_neigh, load_sem, store_sem):
    loads = [
        pltpu.make_async_copy(src, via, load_sem.at[i])
        for i, (src, via) in enumerate(((w_in, w_fin), (out_in, out), (grad_in, grad)))]
    stores = [
        pltpu.make_async_copy(via, dst, store_sem.at[i])
        for i, (via, dst) in enumerate(((grad_self, self_to), (grad_neigh, neigh_to), (out, out_to), (grad, grad_to)))]
    for load in loads:
        load.start()
    loads[0].wait()
    _, blocks, crows, _ = w_fin.shape
    nx = blocks // ny
    for matrix, result in enumerate((grad_self, grad_neigh)):
        for j in range(nx):
            for i in range(ny):
                top = (i * (nx // 2) + j // 2) * crows
                result[top:top + crows, (j % 2) * 128:(j % 2) * 128 + 128] = w_fin[matrix, j * ny + i].astype(F32)
        stores[matrix].start()
        loads[matrix + 1].wait()
        stores[matrix + 2].start()
    for copy in stores:
        copy.wait()


def on_device(dims, features, w_self, w_neigh, adjacency, tile_ids, send_rows, send_counts, hub_rows, cotangent):
    nd, ny, nz, nx = dims
    nodes, width = features.shape
    row_tiles, _, tile, _ = adjacency.shape
    slots, hubs = send_rows.shape[1], hub_rows.shape[1]
    src_tiles = (nodes + nd * slots + nz * nx * hubs) // tile
    crows = nodes // ny // (nx // 2)
    args = (features, w_self, w_neigh, adjacency, tile_ids, send_rows, send_counts, hub_rows, cotangent)
    hbm = pl.BlockSpec(memory_space=pltpu.HBM)
    dma = pltpu.SemaphoreType.DMA
    results = pl.pallas_call(
        functools.partial(kernel, dims),
        out_shape=(
            jax.ShapeDtypeStruct((nodes, width), BF16),
            jax.ShapeDtypeStruct((nodes, width), BF16),
            jax.ShapeDtypeStruct((2, nx * ny, crows, 128), BF16),
        ),
        in_specs=[hbm] * len(args),
        out_specs=[hbm] * 3,
        scratch_shapes=[
            (pltpu.SMEM if arg is tile_ids else pltpu.VMEM)(arg.shape, arg.dtype) for arg in args
        ] + [
            dma((len(args),)),
            pltpu.VMEM((nodes, width), BF16),
            pltpu.VMEM((nodes, width), BF16),
            dma((4,)),
            pltpu.VMEM((nd, slots, width), BF16),
            pltpu.VMEM((nd, slots, width), BF16),
            pltpu.VMEM((hubs, width), BF16),
            pltpu.VMEM((nx, nz, hubs, width), BF16),
            pltpu.VMEM((src_tiles, nodes, tile), BF16),
            pltpu.VMEM((src_tiles, tile, nodes), BF16),
            pltpu.VMEM((src_tiles, nodes, tile), BF16),
            pltpu.VMEM((src_tiles, tile, nodes), BF16),
            pltpu.VMEM((nd * slots, nodes), BF16),
            pltpu.VMEM((nodes, nd * slots), BF16),
            pltpu.VMEM((2, width, nodes), BF16),
            pltpu.VMEM((nd, slots, width), BF16),
            pltpu.VMEM((nd, slots, width), BF16),
            pltpu.VMEM((nx, nz, hubs, width), BF16),
            pltpu.VMEM((nx, nz, hubs, width), BF16),
            pltpu.VMEM((nz, hubs, width), BF16),
            pltpu.VMEM((nz, hubs, width), BF16),
            pltpu.VMEM((width, width), F32),
            pltpu.VMEM((width, width), F32),
            pltpu.VMEM((ny * nx, crows, 128), BF16),
            pltpu.VMEM((ny * nx, crows, 128), BF16),
            pltpu.VMEM((nz, crows, 128), BF16),
            pltpu.VMEM((2, nx * ny, crows, 128), BF16),
        ] + [dma] * 3 + [dma((3,))] + [dma] * 18,
        compiler_params=pltpu.CompilerParams(
            collective_id=0, has_side_effects=True, vmem_limit_bytes=VMEM_LIMIT),
    )(*args)
    rows = jax.ShapeDtypeStruct((nodes, width), BF16)
    weights = jax.ShapeDtypeStruct((width, width), F32)
    return pl.pallas_call(
        functools.partial(store, ny),
        out_shape=(rows, rows, weights, weights),
        in_specs=[hbm] * 3,
        out_specs=[hbm] * 4,
        scratch_shapes=[pltpu.VMEM(r.shape, r.dtype) for r in (*results, weights, weights)] + [dma((3,)), dma((4,))],
        compiler_params=pltpu.CompilerParams(vmem_limit_bytes=VMEM_LIMIT),
    )(*results)


def solution(mesh):
    nd, ng = mesh.shape["dom"], mesh.shape["grp"]
    dims = (nd, nd // CORES, ng // X_CHIPS, X_CHIPS)
    placed = (
        P(("dom", "grp"), None),
        P(),
        P(),
        P(("dom", "grp"), None, None, None),
        P(("dom", "grp"), None),
        P(("dom", "grp"), None),
        P(("dom", "grp"), None),
        P(("dom", "grp"), None),
        P(("dom", "grp"), None),
    )
    return jax.shard_map(
        functools.partial(on_device, dims),
        mesh=mesh,
        in_specs=placed,
        out_specs=(P(("dom", "grp"), None), P(("dom", "grp"), None), P(), P()),
        check_vma=False,
    )
```
